512 devices in a mesh: lat: 32 (over z, y_lo), lon: 16 (over y_hi, x, core).
Axes of the slice: x: 4, y: 4 (y_hi: 2, y_lo: 2; y = y_hi * 2 + y_lo), z: 16, core: 2. Of those that a mesh axis runs over, the one named last changes fastest.
Arguments:
- grid_state: bfloat16 [1, 128, 1024, 1024], P(None, 'lat', 'lon'), may hold values from -45 to 45
- stencil_one: float32 [2, 3, 1024], replicated, may hold values from -1.5 to 1.5
- stencil_two: float32 [2, 3, 1024], replicated, may hold values from -1.5 to 1.5
- norm_gain: float32 [1024], replicated, may hold values from 0.5 to 1.5
- query_weight: bfloat16 [1024, 1024], replicated, may hold values from -0.125 to 0.125
- key_value_weight: bfloat16 [1024, 512], replicated, may hold values from -3.125 to 3.125
Outputs:
- mixed_field: bfloat16 [1, 128, 1024, 1024], P(None, 'lat', 'lon')
- attended: bfloat16 [1, 128, 1024, 1024], P(None, 'lat', 'lon')
The draws below stay inside these ranges and needn't reach their ends.
All inputs are finite; a program needn't handle non-finite values.
Results may differ from the reference program's by a relative error of at most 0.035.
Values may be sent and summed in bfloat16 or wider, within the bound.
No kernel may reach another device: no remote copies, remote signals or barrier semaphores. Data moves between devices by JAX's collectives and lax.ppermute only.
A program may use at most 64 MiB of HBM per device.

```python
import math
import jax
import jax.numpy as jnp
from jax import lax

D = 1024
HEADS = 16
KV_HEADS = 4
HEAD_DIM = 64
LEVELS = 1
NLON = 1024
NLAT = 128


def draw_grid_state(key, part):
    key = jax.random.fold_in(key, 11)
    base_key, row_key, column_key = jax.random.split(key, 3)
    base = jnp.clip(jax.random.normal(base_key, (LEVELS, NLAT, NLON, D), jnp.float32), -4.0, 4.0)
    row_scale = jnp.exp(jax.random.uniform(row_key, (LEVELS, NLAT, NLON, 1), jnp.float32, -1.15, 1.15))
    column_scale = jnp.exp(jax.random.uniform(column_key, (1, 1, 1, D), jnp.float32, -1.15, 1.15))
    return (base * row_scale * column_scale).astype(jnp.bfloat16)


def draw_query_weight(key, part):
    key = jax.random.fold_in(key, 12)
    own = jnp.clip(jax.random.normal(key, (D, HEADS * HEAD_DIM), jnp.float32), -4.0, 4.0) / math.sqrt(D)
    return own.astype(jnp.bfloat16)


def draw_key_value_weight(key, part):
    key = jax.random.fold_in(key, 13)
    key_width = KV_HEADS * HEAD_DIM
    own = jnp.clip(jax.random.normal(key, (D, 2 * key_width), jnp.float32), -4.0, 4.0) / math.sqrt(D)
    return own.astype(jnp.bfloat16)


def gaussian(rng, shape, width, reach, kind=jnp.bfloat16):
    return jnp.clip(width * jax.random.normal(rng, shape, jnp.float32), -reach, reach).astype(kind)


def setup_inputs(seed: int = 0) -> dict:
    arg_keys = jax.random.split(jax.random.key(seed), 7)
    return {
        "grid_state": draw_grid_state(jax.random.fold_in(arg_keys[6], 71), 0),
        "stencil_one": gaussian(arg_keys[1], (2, 3, D), 0.3, 1.5, jnp.float32),
        "stencil_two": gaussian(arg_keys[2], (2, 3, D), 0.3, 1.5, jnp.float32),
        "norm_gain": jnp.clip(1.0 + 0.1 * jax.random.normal(arg_keys[3], (D,), jnp.float32), 0.5, 1.5),
        "query_weight": draw_query_weight(jax.random.fold_in(arg_keys[6], 71), 0),
        "key_value_weight": draw_key_value_weight(jax.random.fold_in(arg_keys[6], 71), 0),
    }


def band_weights(first_row, row_count, nlat_total):
    positions = (jnp.arange(row_count, dtype=jnp.int32) + first_row).astype(jnp.float32)
    return jnp.abs(jnp.sin(jnp.pi * (positions + 0.5) / nlat_total))

def apply_stencil(extended, weights, row_weights):
    scaled = extended.astype(jnp.float32) * row_weights[None, :, None, None]
    column_count = extended.shape[2] - 2
    running = jnp.zeros_like(scaled[:, 1:-1, 1:-1])
    for offset in range(3):
        centre = scaled[:, 1:-1, offset:offset + column_count]
        beside = scaled[:, :-2, offset:offset + column_count] + scaled[:, 2:, offset:offset + column_count]
        running = running + weights[0, offset] * centre + weights[1, offset] * beside
    return (extended[:, 1:-1, 1:-1].astype(jnp.float32) + running).astype(jnp.bfloat16)

def extend_whole(layer_input):
    half_circle = layer_input.shape[2] // 2
    upper_rim = jnp.roll(layer_input[:, :1], -half_circle, axis=2)
    lower_rim = jnp.roll(layer_input[:, -1:], -half_circle, axis=2)
    band_rows = jnp.concatenate([upper_rim, layer_input, lower_rim], axis=1)
    return jnp.concatenate([band_rows[:, :, -1:], band_rows, band_rows[:, :, :1]], axis=2)

def circle_rows(packed):
    query_row, key_row, value_row = packed
    groups = HEADS // KV_HEADS
    queries = query_row.reshape(NLON, HEADS, HEAD_DIM).astype(jnp.float32)
    keys_full = jnp.repeat(key_row.reshape(NLON, KV_HEADS, HEAD_DIM), groups, axis=1).astype(jnp.float32)
    values_full = jnp.repeat(value_row.reshape(NLON, KV_HEADS, HEAD_DIM), groups, axis=1).astype(jnp.float32)
    scores = jnp.einsum('qhd,khd->hqk', queries, keys_full) / math.sqrt(HEAD_DIM)
    row_peak = lax.optimization_barrier(jnp.max(scores, axis=-1, keepdims=True))
    exponent = jnp.exp(scores - row_peak)
    denominator = lax.optimization_barrier(jnp.sum(exponent, axis=-1))
    probs = exponent.astype(jnp.bfloat16).astype(jnp.float32)
    mixed = jnp.einsum('hqk,khd->qhd', probs, values_full) / jnp.transpose(denominator)[:, :, None]
    return mixed.reshape(NLON, HEADS * HEAD_DIM).astype(jnp.bfloat16)

def reference(grid_state, stencil_one, stencil_two, norm_gain, query_weight, key_value_weight):
    row_weights = band_weights(-1, NLAT + 2, NLAT)
    after_one = apply_stencil(extend_whole(grid_state), stencil_one, row_weights)
    mixed_field = apply_stencil(extend_whole(after_one), stencil_two, row_weights)
    flattened = mixed_field.reshape(LEVELS * NLAT * NLON, D).astype(jnp.float32)
    mean_square = lax.optimization_barrier(jnp.mean(flattened * flattened, axis=-1, keepdims=True))
    normed = (flattened * lax.rsqrt(mean_square + 1e-06) * norm_gain).astype(jnp.bfloat16)
    queries = jnp.dot(normed, query_weight, preferred_element_type=jnp.float32).astype(jnp.bfloat16)
    key_values = jnp.dot(normed, key_value_weight, preferred_element_type=jnp.float32).astype(jnp.bfloat16)
    queries = queries.reshape(LEVELS * NLAT, NLON, D)
    key_values = key_values.reshape(LEVELS * NLAT, NLON, 2 * KV_HEADS * HEAD_DIM)
    key_width = KV_HEADS * HEAD_DIM
    attended = lax.map(circle_rows, (queries, key_values[..., :key_width], key_values[..., key_width:]))
    return (mixed_field, attended.reshape(LEVELS, NLAT, NLON, D))
```

```python
import jax
import jax.numpy as jnp
from jax import lax
from jax.experimental import pallas as pl
from jax.experimental.pallas import tpu as pltpu
from jax.sharding import PartitionSpec as P

HEADS = 16
KV_HEADS = 4
HEAD_DIM = 64
GROUPS = HEADS // KV_HEADS
QW = GROUPS * HEAD_DIM
SLOT = QW + 2 * HEAD_DIM


def meridian_pairs(bands, columns, west_north):
    half = columns // 2
    pairs = []
    for i in range(bands):
        for j in range(columns):
            if (j < half) == west_north:
                to = (i - 1, j) if i > 0 else (0, (j + half) % columns)
            else:
                to = (i + 1, j) if i < bands - 1 else (bands - 1, (j + half) % columns)
            pairs.append((i * columns + j, to[0] * columns + to[1]))
    return pairs


def extend(u):
    bands, columns = lax.axis_size("lat"), lax.axis_size("lon")
    lat, lon = lax.axis_index("lat"), lax.axis_index("lon")
    west = lon < columns // 2
    head, tail = u[:2], u[-2:]
    a = lax.ppermute(
        jnp.where(west, head, tail), ("lat", "lon"), meridian_pairs(bands, columns, True)
    )
    b = lax.ppermute(
        jnp.where(west, tail, head), ("lat", "lon"), meridian_pairs(bands, columns, False)
    )
    lower, upper = jnp.where(west, a, b), jnp.where(west, b, a)
    lower = jnp.where(lat == bands - 1, lower[::-1], lower)
    upper = jnp.where(lat == 0, upper[::-1], upper)
    rows = jnp.concatenate([upper, u, lower], axis=0)
    even = lon % 2 == 0
    left_edge, right_edge = rows[:, :2], rows[:, -2:]
    sib = lax.ppermute(
        jnp.where(even, right_edge, left_edge), "lon", [(j, j ^ 1) for j in range(columns)]
    )
    cross = lax.ppermute(
        jnp.where(even, left_edge, right_edge),
        "lon",
        [(j, (j + (1 if j % 2 else -1)) % columns) for j in range(columns)],
    )
    left, right = jnp.where(even, cross, sib), jnp.where(even, sib, cross)
    return jnp.concatenate([left, rows, right], axis=1)


def row_weights(first_row, row_count, nlat):
    positions = (jnp.arange(row_count, dtype=jnp.int32) + first_row).astype(jnp.float32)
    return jnp.abs(jnp.sin(jnp.pi * (positions + 0.5) / nlat))


def apply_stencil(extended, weights, c):
    scaled = extended.astype(jnp.float32) * c[:, None, None]
    n = extended.shape[1] - 2
    running = jnp.zeros_like(scaled[1:-1, 1:-1])
    for b in range(3):
        centre = scaled[1:-1, b : b + n]
        beside = scaled[:-2, b : b + n] + scaled[2:, b : b + n]
        running = running + weights[0, b] * centre + weights[1, b] * beside
    return (extended[1:-1, 1:-1].astype(jnp.float32) + running).astype(jnp.bfloat16)


def attention_kernel(x_ref, o_ref):
    n = x_ref.shape[0]
    k = x_ref[:, QW : QW + HEAD_DIM]
    v = x_ref[:, QW + HEAD_DIM :]
    ones = jnp.ones((n, HEAD_DIM), jnp.bfloat16)
    v_ext = jnp.concatenate([v, ones], axis=1)
    block = 256
    for i in range(n // block):
        outs = []
        for h in range(GROUPS):
            q = x_ref[i * block : (i + 1) * block, h * HEAD_DIM : (h + 1) * HEAD_DIM]
            q = q * jnp.bfloat16(HEAD_DIM**-0.5)
            s = lax.dot_general(
                q, k, (((1,), (1,)), ((), ())), preferred_element_type=jnp.float32
            )
            p = jnp.exp(s - jnp.max(s, axis=1, keepdims=True)).astype(jnp.bfloat16)
            o = jnp.dot(p, v_ext, preferred_element_type=jnp.float32)
            outs.append(o[:, :HEAD_DIM] / o[:, HEAD_DIM:])
        o_ref[i * block : (i + 1) * block, :] = jnp.concatenate(outs, axis=1).astype(jnp.bfloat16)


def attention(x):
    n = x.shape[0]
    return pl.pallas_call(
        attention_kernel,
        out_shape=jax.ShapeDtypeStruct((n, QW), jnp.bfloat16),
        in_specs=[pl.BlockSpec(memory_space=pltpu.VMEM)],
        out_specs=pl.BlockSpec(memory_space=pltpu.VMEM),
        compiler_params=pltpu.CompilerParams(vmem_limit_bytes=48 * 1024 * 1024),
        cost_estimate=pl.CostEstimate(
            flops=4 * GROUPS * n * n * HEAD_DIM,
            bytes_accessed=2 * n * (SLOT + QW),
            transcendentals=GROUPS * n * n,
        ),
        name="attention",
    )(x)


def local(grid_state, stencil_one, stencil_two, norm_gain, query_weight, key_value_weight):
    _, rows, cols, channels = grid_state.shape
    nlat = rows * lax.axis_size("lat")
    first = lax.axis_index("lat") * rows
    c = row_weights(first - 2, rows + 4, nlat)
    after_one = apply_stencil(extend(grid_state[0]), stencil_one, c)
    mixed_field = apply_stencil(after_one, stencil_two, c[1:-1])
    flat = mixed_field.reshape(rows * cols, channels).astype(jnp.float32)
    mean_square = jnp.mean(flat * flat, axis=-1, keepdims=True)
    normed = (flat * lax.rsqrt(mean_square + 1e-06) * norm_gain).astype(jnp.bfloat16)
    kw = KV_HEADS * HEAD_DIM
    weight = jnp.concatenate(
        [
            query_weight.reshape(channels, KV_HEADS, QW),
            key_value_weight[:, :kw].reshape(channels, KV_HEADS, HEAD_DIM),
            key_value_weight[:, kw:].reshape(channels, KV_HEADS, HEAD_DIM),
        ],
        axis=2,
    ).reshape(channels, KV_HEADS * SLOT)
    qkv = jnp.dot(normed, weight, preferred_element_type=jnp.float32).astype(jnp.bfloat16)
    slots = (
        qkv.reshape(rows, cols, KV_HEADS, SLOT)
        .transpose(0, 2, 1, 3)
        .reshape(rows * KV_HEADS, cols, SLOT)
    )
    circle = lax.all_to_all(slots, "lon", 0, 0, tiled=True)
    mixed = attention(circle.reshape(-1, SLOT))
    back = lax.all_to_all(mixed.reshape(-1, cols, QW), "lon", 0, 0, tiled=True)
    attended = (
        back.reshape(rows, KV_HEADS, cols, QW)
        .transpose(0, 2, 1, 3)
        .reshape(1, rows, cols, channels)
    )
    return mixed_field[None], attended


def solution(mesh):
    spec = P(None, "lat", "lon", None)
    return jax.shard_map(
        local,
        mesh=mesh,
        in_specs=(spec, P(), P(), P(), P(), P()),
        out_specs=(spec, spec),
        check_vma=False,
    )
```

```python
import math

import jax
import jax.numpy as jnp
from jax import lax
from jax.experimental import pallas as pl
from jax.experimental.pallas import tpu as pltpu
from jax.sharding import PartitionSpec as P

HEADS = 16
KV_HEADS = 4
HEAD_DIM = 64
GROUPS = HEADS // KV_HEADS
QW = GROUPS * HEAD_DIM
SLOT = QW + 2 * HEAD_DIM
MARGIN = 2
LANES = 128
VMEM_LIMIT = 24 * 1024 * 1024


def meridian_pairs(bands, columns, west_north):
    half = columns // 2
    pairs = []
    for i in range(bands):
        for j in range(columns):
            if (j < half) == west_north:
                to = (i - 1, j) if i > 0 else (0, (j + half) % columns)
            else:
                to = (i + 1, j) if i < bands - 1 else (bands - 1, (j + half) % columns)
            pairs.append((i * columns + j, to[0] * columns + to[1]))
    return pairs


def row_weights(first_row, row_count, nlat):
    positions = (jnp.arange(row_count, dtype=jnp.int32) + first_row).astype(jnp.float32)
    return jnp.abs(jnp.sin(jnp.pi * (positions + 0.5) / nlat))


def add_stencil(before, here, after, raw, w_ref, lanes):
    beside = before + after
    t = [
        w_ref[0, b : b + 1, lanes] * here + w_ref[1, b : b + 1, lanes] * beside for b in range(3)
    ]
    return raw + t[1] + pltpu.roll(t[0], 1, 0) + pltpu.roll(t[2], raw.shape[0] - 1, 0)


def two_stencils(row, count, c_ref, one_ref, two_ref, lanes, store):
    raw = [row(0), row(1)]
    scaled = [raw[0] * c_ref[0], raw[1] * c_ref[1]]
    after, after_scaled = [None], [None]
    for r in range(2, count + 4):
        raw.append(row(r))
        scaled.append(raw[r] * c_ref[r])
        v = add_stencil(scaled[r - 2], scaled[r - 1], scaled[r], raw[r - 1], one_ref, lanes)
        v = v.astype(jnp.bfloat16).astype(jnp.float32)
        after.append(v)
        after_scaled.append(v * c_ref[r - 1])
        if r >= 4:
            store(
                r - 4,
                add_stencil(
                    after_scaled[r - 3],
                    after_scaled[r - 2],
                    after_scaled[r - 1],
                    after[r - 2],
                    two_ref,
                    lanes,
                ),
            )


def inner_kernel(c_ref, flag_ref, u_ref, a_ref, b_ref, one_ref, two_ref, mixed_ref, side_ref):
    rows, cols, channels = u_ref.shape
    west = flag_ref[0] == 1
    north, south = flag_ref[1], flag_ref[2]

    def chunk(n, _):
        lanes = pl.ds(pl.multiple_of(n * LANES, LANES), LANES)

        def row(r):
            if 2 <= r < rows + 2:
                main = u_ref[r - 2, :, lanes].astype(jnp.float32)
            elif r < 2:
                i = jnp.where(north == 1, 1 - r, r)
                main = jnp.where(
                    west,
                    b_ref[i, :, lanes].astype(jnp.float32),
                    a_ref[i, :, lanes].astype(jnp.float32),
                )
            else:
                i = jnp.where(south == 1, rows + 3 - r, r - rows - 2)
                main = jnp.where(
                    west,
                    a_ref[i, :, lanes].astype(jnp.float32),
                    b_ref[i, :, lanes].astype(jnp.float32),
                )
            side_ref[r, :, lanes] = main[cols - 8 :].astype(jnp.bfloat16)
            return main

        def store(r, v):
            mixed_ref[r, :, lanes] = v.astype(jnp.bfloat16)

        two_stencils(row, rows, c_ref, one_ref, two_ref, lanes, store)
        return 0

    lax.fori_loop(0, channels // LANES, chunk, 0)


def inner(c, flags, u, a, b, one, two):
    rows, cols, channels = u.shape
    vmem, smem = pl.BlockSpec(memory_space=pltpu.VMEM), pl.BlockSpec(memory_space=pltpu.SMEM)
    return pl.pallas_call(
        inner_kernel,
        out_shape=(
            jax.ShapeDtypeStruct((rows, cols, channels), jnp.bfloat16),
            jax.ShapeDtypeStruct((rows + 4, 8, channels), jnp.bfloat16),
        ),
        in_specs=[smem, smem] + [vmem] * 5,
        out_specs=(vmem, vmem),
        compiler_params=pltpu.CompilerParams(vmem_limit_bytes=VMEM_LIMIT),
        cost_estimate=pl.CostEstimate(
            flops=40 * rows * cols * channels, bytes_accessed=8 * 1024 * 1024, transcendentals=0
        ),
        name="inner",
    )(c, flags, u, a, b, one, two)


def project_kernel(
    c_ref,
    side_ref,
    edge_ref,
    inner_ref,
    one_ref,
    two_ref,
    gain_ref,
    wq,
    wkv,
    mixed_ref,
    slots_ref,
    strip,
    normed,
):
    rows, cols, channels = inner_ref.shape
    margin = edge_ref.shape[1]
    pad = jnp.zeros((8 - margin, LANES), jnp.float32)

    def chunk(n, _):
        lanes = pl.ds(pl.multiple_of(n * LANES, LANES), LANES)

        def row(r):
            return jnp.concatenate(
                [
                    side_ref[r, :, lanes].astype(jnp.float32),
                    edge_ref[r, :, lanes].astype(jnp.float32),
                    pad,
                ],
                axis=0,
            )

        def store(r, v):
            strip[r, :, lanes] = v

        two_stencils(row, rows, c_ref, one_ref, two_ref, lanes, store)
        return 0

    lax.fori_loop(0, channels // LANES, chunk, 0, unroll=2)
    place = lax.broadcasted_iota(jnp.int32, (8, channels), 0)
    for r in range(rows):
        m = inner_ref[r].astype(jnp.float32)
        m = jnp.concatenate(
            [
                jnp.where(place < MARGIN, strip[r, 8:], m[:8]),
                m[8 : cols - 8],
                jnp.where(place >= 8 - MARGIN, strip[r, :8], m[cols - 8 :]),
            ],
            axis=0,
        ).astype(jnp.bfloat16)
        mixed_ref[r] = m
        m = m.astype(jnp.float32)
        mean_square = jnp.sum(m * m, axis=1, keepdims=True) * (1.0 / channels)
        normed[r * cols : (r + 1) * cols, :] = (
            m * lax.rsqrt(mean_square + 1e-06) * gain_ref[...]
        ).astype(jnp.bfloat16)
    x = normed[...]
    kv = jnp.dot(x, wkv[...], preferred_element_type=jnp.float32).astype(jnp.bfloat16)
    kw = KV_HEADS * HEAD_DIM
    for g in range(KV_HEADS):
        q = jnp.dot(x, wq[:, g * QW : (g + 1) * QW], preferred_element_type=jnp.float32)
        q = (q * (math.log2(math.e) / math.sqrt(HEAD_DIM))).astype(jnp.bfloat16)
        at = g * HEAD_DIM
        pair = jnp.concatenate(
            [kv[:, at : at + HEAD_DIM], kv[:, kw + at : kw + at + HEAD_DIM]], axis=1
        )
        for r in range(rows):
            here = slice(r * cols, (r + 1) * cols)
            slots_ref[r * KV_HEADS + g, :, :QW] = q[here]
            slots_ref[r * KV_HEADS + g, :, QW:] = pair[here]


def project(c, side, edge, mixed, one, two, gain, wq, wkv):
    rows, cols, channels = mixed.shape
    vmem, smem = pl.BlockSpec(memory_space=pltpu.VMEM), pl.BlockSpec(memory_space=pltpu.SMEM)
    return pl.pallas_call(
        project_kernel,
        out_shape=(
            jax.ShapeDtypeStruct((rows, cols, channels), jnp.bfloat16),
            jax.ShapeDtypeStruct((rows * KV_HEADS, cols, SLOT), jnp.bfloat16),
        ),
        in_specs=[smem] + [vmem] * 8,
        out_specs=(vmem, vmem),
        scratch_shapes=[
            pltpu.VMEM((rows, 16, channels), jnp.float32),
            pltpu.VMEM((rows * cols, channels), jnp.bfloat16),
        ],
        compiler_params=pltpu.CompilerParams(vmem_limit_bytes=VMEM_LIMIT),
        cost_estimate=pl.CostEstimate(
            flops=3 * rows * cols * channels * channels,
            bytes_accessed=6 * 1024 * 1024,
            transcendentals=0,
        ),
        name="project",
    )(c, side, edge, mixed, one, two, gain, wq, wkv)


def attention_kernel(x_ref, o_ref):
    blocks, cols, _ = o_ref.shape
    n = blocks * cols
    k = x_ref[:, QW : QW + HEAD_DIM]
    ones = jnp.ones((n, HEAD_DIM), jnp.bfloat16)
    v = jnp.concatenate([x_ref[:, QW + HEAD_DIM :], ones], axis=1)
    step = n // 2
    for i in range(0, n, step):
        outs = []
        for h in range(GROUPS):
            q = x_ref[i : i + step, h * HEAD_DIM : (h + 1) * HEAD_DIM]
            s = lax.dot_general(
                q, k, (((1,), (1,)), ((), ())), preferred_element_type=jnp.float32
            )
            p = jnp.exp2(s - jnp.max(s, axis=1, keepdims=True)).astype(jnp.bfloat16)
            o = jnp.dot(p, v, preferred_element_type=jnp.float32)
            outs.append(o[:, :HEAD_DIM] / o[:, HEAD_DIM:])
        o = jnp.concatenate(outs, axis=1).astype(jnp.bfloat16)
        o_ref[i // cols : (i + step) // cols] = o.reshape(step // cols, cols, QW)
    tile = 16
    heads = [o_ref[b, :tile, :] for b in range(blocks)]
    moved = lax.broadcasted_iota(jnp.int32, (tile, QW), 0) < MARGIN
    for b in range(blocks):
        o_ref[b, :tile, :] = jnp.where(moved, heads[b - 1], heads[b])


def attention(x, blocks):
    n = x.shape[0]
    return pl.pallas_call(
        attention_kernel,
        out_shape=jax.ShapeDtypeStruct((blocks, n // blocks, QW), jnp.bfloat16),
        in_specs=[pl.BlockSpec(memory_space=pltpu.VMEM)],
        out_specs=pl.BlockSpec(memory_space=pltpu.VMEM),
        compiler_params=pltpu.CompilerParams(vmem_limit_bytes=VMEM_LIMIT),
        cost_estimate=pl.CostEstimate(
            flops=4 * GROUPS * n * n * HEAD_DIM,
            bytes_accessed=2 * n * (SLOT + QW),
            transcendentals=GROUPS * n * n,
        ),
        name="attention",
    )(x)


def gather_heads_kernel(x_ref, o_ref):
    for g in range(KV_HEADS):
        o_ref[0, :, g * QW : (g + 1) * QW] = x_ref[g]


def gather_heads(x, rows, cols, channels):
    return pl.pallas_call(
        gather_heads_kernel,
        grid=(rows,),
        out_shape=jax.ShapeDtypeStruct((rows, cols, channels), jnp.bfloat16),
        in_specs=[pl.BlockSpec((KV_HEADS, cols, QW), lambda r: (r, 0, 0))],
        out_specs=pl.BlockSpec((1, cols, channels), lambda r: (r, 0, 0)),
        compiler_params=pltpu.CompilerParams(vmem_limit_bytes=VMEM_LIMIT),
        name="gather_heads",
    )(x)


def local(grid_state, stencil_one, stencil_two, norm_gain, query_weight, key_value_weight):
    u = grid_state[0]
    rows, cols, channels = u.shape
    bands, columns = lax.axis_size("lat"), lax.axis_size("lon")
    lat, lon = lax.axis_index("lat"), lax.axis_index("lon")
    c = row_weights(lat * rows - 2, rows + 4, rows * bands)
    west = lon < columns // 2
    first, last = lat == 0, lat == bands - 1

    def towards(west_north):
        start = jnp.where(west == west_north, 0, rows - 2)
        return lax.ppermute(
            lax.dynamic_slice_in_dim(u, start, 2, axis=0),
            ("lat", "lon"),
            meridian_pairs(bands, columns, west_north),
        )

    a, b = towards(True), towards(False)

    ea, eb, eu = a[:, : 2 * MARGIN], b[:, : 2 * MARGIN], u[:, : 2 * MARGIN]
    lower, upper = jnp.where(west, ea, eb), jnp.where(west, eb, ea)
    lower = jnp.where(last, lower[::-1], lower)
    upper = jnp.where(first, upper[::-1], upper)
    edge = lax.ppermute(
        jnp.concatenate([upper, eu, lower], axis=0),
        "lon",
        [(j, (j - 1) % columns) for j in range(columns)],
    )
    flags = jnp.stack([west, first, last]).astype(jnp.int32)
    mixed_inner, side = inner(c, flags, u, a, b, stencil_one, stencil_two)
    mixed_field, slots = project(
        c,
        side,
        edge,
        mixed_inner,
        stencil_one,
        stencil_two,
        norm_gain[None],
        query_weight,
        key_value_weight,
    )
    circle = lax.all_to_all(slots, "lon", 0, 0, tiled=True)
    displaced = lax.ppermute(
        mixed_field[:, :MARGIN], "lon", [(j, (j + 1) % columns) for j in range(columns)]
    )
    mixed_field = lax.dynamic_update_slice(mixed_field, displaced, (0, 0, 0))
    circle, mixed_field = lax.optimization_barrier((circle, mixed_field))
    back = attention(circle.reshape(-1, SLOT), columns)
    back = lax.all_to_all(back, "lon", 0, 0, tiled=True)
    attended = gather_heads(back, rows, cols, channels)
    return mixed_field[None], attended[None]


def solution(mesh):
    spec = P(None, "lat", "lon", None)
    return jax.shard_map(
        local,
        mesh=mesh,
        in_specs=(spec, P(), P(), P(), P(), P()),
        out_specs=(spec, spec),
        check_vma=False,
    )
```

```python
import math

import jax
import jax.numpy as jnp
from jax import lax
from jax.experimental import pallas as pl
from jax.experimental.pallas import tpu as pltpu
from jax.sharding import PartitionSpec as P

HEADS = 16
KV_HEADS = 4
HEAD_DIM = 64
GROUPS = HEADS // KV_HEADS
QW = GROUPS * HEAD_DIM
SLOT = QW + 2 * HEAD_DIM
MARGIN = 2
LANES = 128
VMEM_LIMIT = 24 * 1024 * 1024


def meridian_pairs(bands, columns, west_north):
    half = columns // 2
    pairs = []
    for i in range(bands):
        for j in range(columns):
            if (j < half) == west_north:
                to = (i - 1, j) if i > 0 else (0, (j + half) % columns)
            else:
                to = (i + 1, j) if i < bands - 1 else (bands - 1, (j + half) % columns)
            pairs.append((i * columns + j, to[0] * columns + to[1]))
    return pairs


def row_weights(first_row, row_count, nlat):
    positions = (jnp.arange(row_count, dtype=jnp.int32) + first_row).astype(jnp.float32)
    return jnp.abs(jnp.sin(jnp.pi * (positions + 0.5) / nlat))


def add_stencil(before, here, after, raw, w_ref, lanes):
    beside = before + after
    t = [
        w_ref[0, b : b + 1, lanes] * here + w_ref[1, b : b + 1, lanes] * beside for b in range(3)
    ]
    return raw + t[1] + pltpu.roll(t[0], 1, 0) + pltpu.roll(t[2], raw.shape[0] - 1, 0)


def two_stencils(row, count, c_ref, one_ref, two_ref, lanes, store):
    raw = [row(0), row(1)]
    scaled = [raw[0] * c_ref[0], raw[1] * c_ref[1]]
    after, after_scaled = [None], [None]
    for r in range(2, count + 4):
        raw.append(row(r))
        scaled.append(raw[r] * c_ref[r])
        v = add_stencil(scaled[r - 2], scaled[r - 1], scaled[r], raw[r - 1], one_ref, lanes)
        v = v.astype(jnp.bfloat16).astype(jnp.float32)
        after.append(v)
        after_scaled.append(v * c_ref[r - 1])
        if r >= 4:
            store(
                r - 4,
                add_stencil(
                    after_scaled[r - 3],
                    after_scaled[r - 2],
                    after_scaled[r - 1],
                    after[r - 2],
                    two_ref,
                    lanes,
                ),
            )


def inner_kernel(c_ref, flag_ref, u_ref, a_ref, b_ref, one_ref, two_ref, mixed_ref, side_ref):
    rows, cols, channels = u_ref.shape
    west = flag_ref[0] == 1
    north, south = flag_ref[1], flag_ref[2]

    def chunk(n, _):
        lanes = pl.ds(pl.multiple_of(n * LANES, LANES), LANES)

        def row(r):
            if 2 <= r < rows + 2:
                main = u_ref[r - 2, :, lanes]
            elif r < 2:
                i = jnp.where(north == 1, 1 - r, r)
                main = jnp.where(
                    west,
                    b_ref[i, :, lanes].astype(jnp.float32),
                    a_ref[i, :, lanes].astype(jnp.float32),
                )
            else:
                i = jnp.where(south == 1, rows + 3 - r, r - rows - 2)
                main = jnp.where(
                    west,
                    a_ref[i, :, lanes].astype(jnp.float32),
                    b_ref[i, :, lanes].astype(jnp.float32),
                )
            side_ref[r, :, lanes] = main[cols - 8 :].astype(jnp.bfloat16)
            return main

        def store(r, v):
            mixed_ref[r, :, lanes] = v.astype(jnp.bfloat16)

        two_stencils(row, rows, c_ref, one_ref, two_ref, lanes, store)
        return 0

    lax.fori_loop(0, channels // LANES, chunk, 0)


def inner(c, flags, u, a, b, one, two):
    rows, cols, channels = u.shape
    vmem, smem = pl.BlockSpec(memory_space=pltpu.VMEM), pl.BlockSpec(memory_space=pltpu.SMEM)
    return pl.pallas_call(
        inner_kernel,
        out_shape=(
            jax.ShapeDtypeStruct((rows, cols, channels), jnp.bfloat16),
            jax.ShapeDtypeStruct((rows + 4, 8, channels), jnp.bfloat16),
        ),
        in_specs=[smem, smem] + [vmem] * 5,
        out_specs=(vmem, vmem),
        compiler_params=pltpu.CompilerParams(vmem_limit_bytes=VMEM_LIMIT),
        cost_estimate=pl.CostEstimate(
            flops=40 * rows * cols * channels, bytes_accessed=8 * 1024 * 1024, transcendentals=0
        ),
        name="inner",
    )(c, flags, u, a, b, one, two)


def project_kernel(
    c_ref,
    side_ref,
    edge_ref,
    inner_ref,
    one_ref,
    two_ref,
    gain_ref,
    wkv,
    wq0,
    wq1,
    wq2,
    wq3,
    mixed_hbm,
    slots_hbm,
    head_ref,
    mixed_ref,
    slots_ref,
    strip,
    normed,
    sems,
    slot_sems,
):
    rows, cols, channels = inner_ref.shape
    margin = edge_ref.shape[1]
    pad = jnp.zeros((8 - margin, LANES), jnp.float32)

    def chunk(n, _):
        lanes = pl.ds(pl.multiple_of(n * LANES, LANES), LANES)

        def row(r):
            return jnp.concatenate(
                [
                    side_ref[r, :, lanes].astype(jnp.float32),
                    edge_ref[r, :, lanes].astype(jnp.float32),
                    pad,
                ],
                axis=0,
            )

        def store(r, v):
            strip[r, :, lanes] = v

        two_stencils(row, rows, c_ref, one_ref, two_ref, lanes, store)
        return 0

    lax.fori_loop(0, channels // LANES, chunk, 0, unroll=2)
    place = lax.broadcasted_iota(jnp.int32, (8, channels), 0)
    copies = []
    for r in range(rows):
        m = inner_ref[r].astype(jnp.float32)
        m = jnp.concatenate(
            [
                jnp.where(place < MARGIN, strip[r, 8:], m[:8]),
                m[8 : cols - 8],
                jnp.where(place >= 8 - MARGIN, strip[r, :8], m[cols - 8 :]),
            ],
            axis=0,
        ).astype(jnp.bfloat16)
        mixed_ref[r] = m
        head_ref[r] = m[: 2 * 8]
        copies.append(pltpu.make_async_copy(mixed_ref.at[r], mixed_hbm.at[r], sems.at[r]))
        copies[r].start()
        m = m.astype(jnp.float32)
        mean_square = jnp.sum(m * m, axis=1, keepdims=True) * (1.0 / channels)
        normed[r * cols : (r + 1) * cols, :] = (
            m * lax.rsqrt(mean_square + 1e-06) * gain_ref[...]
        ).astype(jnp.bfloat16)
    x = normed[...]
    kv = jnp.dot(x, wkv[...], preferred_element_type=jnp.float32).astype(jnp.bfloat16)
    kw = KV_HEADS * HEAD_DIM
    for g, wq in enumerate((wq0, wq1, wq2, wq3)):
        q = jnp.dot(x, wq[...], preferred_element_type=jnp.float32)
        q = (q * (math.log2(math.e) / math.sqrt(HEAD_DIM))).astype(jnp.bfloat16)
        at = g * HEAD_DIM
        pair = jnp.concatenate(
            [kv[:, at : at + HEAD_DIM], kv[:, kw + at : kw + at + HEAD_DIM]], axis=1
        )
        for r in range(rows):
            here = slice(r * cols, (r + 1) * cols)
            slots_ref[r * KV_HEADS + g, :, :QW] = q[here]
            slots_ref[r * KV_HEADS + g, :, QW:] = pair[here]
            at = r * KV_HEADS + g
            copies.append(
                pltpu.make_async_copy(slots_ref.at[at], slots_hbm.at[at], slot_sems.at[at])
            )
            copies[-1].start()
    for copy in copies:
        copy.wait()


def project(c, side, edge, mixed, one, two, gain, wq, wkv):
    rows, cols, channels = mixed.shape
    vmem, smem = pl.BlockSpec(memory_space=pltpu.VMEM), pl.BlockSpec(memory_space=pltpu.SMEM)
    hbm = pl.BlockSpec(memory_space=pltpu.HBM)
    return pl.pallas_call(
        project_kernel,
        out_shape=(
            jax.ShapeDtypeStruct((rows, cols, channels), jnp.bfloat16),
            jax.ShapeDtypeStruct((rows * KV_HEADS, cols, SLOT), jnp.bfloat16),
            jax.ShapeDtypeStruct((rows, 16, channels), jnp.bfloat16),
        ),
        in_specs=[smem] + [vmem] * (7 + KV_HEADS),
        out_specs=(hbm, hbm, vmem),
        scratch_shapes=[
            pltpu.VMEM((rows, cols, channels), jnp.bfloat16),
            pltpu.VMEM((rows * KV_HEADS, cols, SLOT), jnp.bfloat16),
            pltpu.VMEM((rows, 16, channels), jnp.float32),
            pltpu.VMEM((rows * cols, channels), jnp.bfloat16),
            pltpu.SemaphoreType.DMA((rows,)),
            pltpu.SemaphoreType.DMA((rows * KV_HEADS,)),
        ],
        compiler_params=pltpu.CompilerParams(vmem_limit_bytes=VMEM_LIMIT),
        cost_estimate=pl.CostEstimate(
            flops=3 * rows * cols * channels * channels,
            bytes_accessed=6 * 1024 * 1024,
            transcendentals=0,
        ),
        name="project",
    )(c, side, edge, mixed, one, two, gain, wkv, *wq)


def attention_kernel(x_ref, o_ref):
    blocks, cols, _ = o_ref.shape
    n = blocks * cols
    kt = x_ref[:, QW : QW + HEAD_DIM].T
    ones = jnp.ones((n, HEAD_DIM), jnp.bfloat16)
    v = jnp.concatenate([x_ref[:, QW + HEAD_DIM :], ones], axis=1)
    step = n // 2
    work = [(i, h) for i in range(0, n, step) for h in range(GROUPS)]

    def scores(i, h):
        q = x_ref[i : i + step, h * HEAD_DIM : (h + 1) * HEAD_DIM]
        return jnp.dot(q, kt, preferred_element_type=jnp.float32)

    outs, ready = [], scores(*work[0])
    for w, (i, h) in enumerate(work):
        s, ready = ready, scores(*work[w + 1]) if w + 1 < len(work) else None
        p = jnp.exp2(s - jnp.max(s, axis=1, keepdims=True)).astype(jnp.bfloat16)
        o = jnp.dot(p, v, preferred_element_type=jnp.float32)
        outs.append(o[:, :HEAD_DIM] / o[:, HEAD_DIM:])
        if h == GROUPS - 1:
            o = jnp.concatenate(outs, axis=1).astype(jnp.bfloat16)
            o_ref[i // cols : (i + step) // cols] = o.reshape(step // cols, cols, QW)
            outs = []
    tile = 16
    heads = [o_ref[b, :tile, :] for b in range(blocks)]
    moved = lax.broadcasted_iota(jnp.int32, (tile, QW), 0) < MARGIN
    for b in range(blocks):
        o_ref[b, :tile, :] = jnp.where(moved, heads[b - 1], heads[b])


def attention(x, blocks):
    n = x.shape[0]
    return pl.pallas_call(
        attention_kernel,
        out_shape=jax.ShapeDtypeStruct((blocks, n // blocks, QW), jnp.bfloat16),
        in_specs=[pl.BlockSpec(memory_space=pltpu.VMEM)],
        out_specs=pl.BlockSpec(memory_space=pltpu.VMEM),
        compiler_params=pltpu.CompilerParams(vmem_limit_bytes=VMEM_LIMIT),
        cost_estimate=pl.CostEstimate(
            flops=4 * GROUPS * n * n * HEAD_DIM,
            bytes_accessed=2 * n * (SLOT + QW),
            transcendentals=GROUPS * n * n,
        ),
        name="attention",
    )(x)


def gather_heads_kernel(x_ref, head_ref, displaced_ref, _, o_hbm, mixed_hbm, staged, tile, sems):
    rows, margin, channels = displaced_ref.shape
    copies = []
    moved = lax.broadcasted_iota(jnp.int32, (16, channels), 0) < margin
    pad = jnp.zeros((16 - margin, channels), jnp.float32)
    for r in range(rows):
        new = jnp.concatenate([displaced_ref[r].astype(jnp.float32), pad], axis=0)
        tile[r] = jnp.where(moved, new, head_ref[r].astype(jnp.float32)).astype(jnp.bfloat16)
        copies.append(
            pltpu.make_async_copy(tile.at[r], mixed_hbm.at[r, pl.ds(0, 16)], sems.at[rows + r])
        )
        copies[-1].start()
        for g in range(KV_HEADS):
            staged[r, :, g * QW : (g + 1) * QW] = x_ref[r * KV_HEADS + g]
        copies.append(pltpu.make_async_copy(staged.at[r], o_hbm.at[r], sems.at[r]))
        copies[-1].start()
    for copy in copies:
        copy.wait()


def gather_heads(x, head, displaced, mixed):
    rows, cols, channels = mixed.shape
    vmem, hbm = pl.BlockSpec(memory_space=pltpu.VMEM), pl.BlockSpec(memory_space=pltpu.HBM)
    whole = jax.ShapeDtypeStruct((rows, cols, channels), jnp.bfloat16)
    return pl.pallas_call(
        gather_heads_kernel,
        out_shape=(whole, whole),
        in_specs=[vmem, vmem, vmem, hbm],
        out_specs=(hbm, hbm),
        input_output_aliases={3: 1},
        scratch_shapes=[
            pltpu.VMEM((rows, cols, channels), jnp.bfloat16),
            pltpu.VMEM((rows, 16, channels), jnp.bfloat16),
            pltpu.SemaphoreType.DMA((2 * rows,)),
        ],
        compiler_params=pltpu.CompilerParams(vmem_limit_bytes=VMEM_LIMIT),
        name="gather_heads",
    )(x, head, displaced, mixed)


def local(grid_state, stencil_one, stencil_two, norm_gain, query_weight, key_value_weight):
    u = grid_state[0]
    rows, cols, channels = u.shape
    bands, columns = lax.axis_size("lat"), lax.axis_size("lon")
    lat, lon = lax.axis_index("lat"), lax.axis_index("lon")
    c = row_weights(lat * rows - 2, rows + 4, rows * bands)
    west = lon < columns // 2
    first, last = lat == 0, lat == bands - 1

    def rim(west_north):
        start = jnp.where(west == west_north, 0, rows - 2)
        return lax.dynamic_slice_in_dim(u, start, 2, axis=0)

    rim_a, rim_b, u = lax.optimization_barrier((rim(True), rim(False), u))
    a = lax.ppermute(rim_a, ("lat", "lon"), meridian_pairs(bands, columns, True))
    b = lax.ppermute(rim_b, ("lat", "lon"), meridian_pairs(bands, columns, False))

    ea, eb, eu = a[:, : 2 * MARGIN], b[:, : 2 * MARGIN], u[:, : 2 * MARGIN]
    lower, upper = jnp.where(west, ea, eb), jnp.where(west, eb, ea)
    lower = jnp.where(last, lower[::-1], lower)
    upper = jnp.where(first, upper[::-1], upper)
    edge = lax.ppermute(
        jnp.concatenate([upper, eu, lower], axis=0),
        "lon",
        [(j, (j - 1) % columns) for j in range(columns)],
    )
    flags = jnp.stack([west, first, last]).astype(jnp.int32)
    mixed_inner, side = inner(c, flags, u.astype(jnp.float32), a, b, stencil_one, stencil_two)
    mixed_field, slots, head_tile = project(
        c,
        side,
        edge,
        mixed_inner,
        stencil_one,
        stencil_two,
        norm_gain[None],
        [query_weight[:, g * QW : (g + 1) * QW] for g in range(KV_HEADS)],
        key_value_weight,
    )
    circle = lax.all_to_all(slots, "lon", 0, 0, tiled=True)
    displaced = lax.ppermute(
        head_tile[:, :MARGIN], "lon", [(j, (j + 1) % columns) for j in range(columns)]
    )
    circle, displaced = lax.optimization_barrier((circle, displaced))
    back = attention(circle.reshape(-1, SLOT), columns)
    back = lax.all_to_all(back, "lon", 0, 0, tiled=True)
    attended, mixed_field = gather_heads(back, head_tile, displaced, mixed_field)
    return mixed_field[None], attended[None]


def solution(mesh):
    spec = P(None, "lat", "lon", None)
    return jax.shard_map(
        local,
        mesh=mesh,
        in_specs=(spec, P(), P(), P(), P(), P()),
        out_specs=(spec, spec),
        check_vma=False,
    )
```

```python
import math

import jax
import jax.numpy as jnp
from jax import lax
from jax.experimental import pallas as pl
from jax.experimental.pallas import tpu as pltpu
from jax.sharding import PartitionSpec as P

HEADS = 16
KV_HEADS = 4
HEAD_DIM = 64
GROUPS = HEADS // KV_HEADS
QW = GROUPS * HEAD_DIM
SLOT = QW + 2 * HEAD_DIM
MARGIN = 2
STRIP_LANES = 512
UNROLL = 1
LANES = 128
VMEM_LIMIT = 24 * 1024 * 1024


def meridian_pairs(bands, columns, west_north):
    half = columns // 2
    pairs = []
    for i in range(bands):
        for j in range(columns):
            if (j < half) == west_north:
                to = (i - 1, j) if i > 0 else (0, (j + half) % columns)
            else:
                to = (i + 1, j) if i < bands - 1 else (bands - 1, (j + half) % columns)
            pairs.append((i * columns + j, to[0] * columns + to[1]))
    return pairs


def row_weights(first_row, row_count, nlat):
    positions = (jnp.arange(row_count, dtype=jnp.int32) + first_row).astype(jnp.float32)
    return jnp.abs(jnp.sin(jnp.pi * (positions + 0.5) / nlat))


def rims_kernel(west_ref, u_hbm, a_ref, b_ref, sems):
    count = a_ref.shape[0]
    last = u_hbm.shape[0] - count
    west = west_ref[0]
    copies = [
        pltpu.make_async_copy(u_hbm.at[pl.ds(last * (1 - west), count)], a_ref, sems.at[0]),
        pltpu.make_async_copy(u_hbm.at[pl.ds(last * west, count)], b_ref, sems.at[1]),
    ]
    for copy in copies:
        copy.start()
    for copy in copies:
        copy.wait()


def rims(west, u):
    rows, cols, channels = u.shape
    rim = jax.ShapeDtypeStruct((2, cols, channels), jnp.bfloat16)
    vmem = pl.BlockSpec(memory_space=pltpu.VMEM)
    return pl.pallas_call(
        rims_kernel,
        out_shape=(rim, rim),
        in_specs=[pl.BlockSpec(memory_space=pltpu.SMEM), pl.BlockSpec(memory_space=pltpu.HBM)],
        out_specs=(vmem, vmem),
        scratch_shapes=[pltpu.SemaphoreType.DMA((2,))],
        compiler_params=pltpu.CompilerParams(vmem_limit_bytes=VMEM_LIMIT),
        name="rims",
    )(west, u)


def add_stencil(before, here, after, raw, w_ref, lanes):
    beside = before + after
    t = [
        w_ref[0, b : b + 1, lanes] * here + w_ref[1, b : b + 1, lanes] * beside for b in range(3)
    ]
    return raw + t[1] + pltpu.roll(t[0], 1, 0) + pltpu.roll(t[2], raw.shape[0] - 1, 0)


def two_stencils(row, count, c_ref, one_ref, two_ref, lanes, store):
    raw = [row(0), row(1)]
    scaled = [raw[0] * c_ref[0], raw[1] * c_ref[1]]
    after, after_scaled = [None], [None]
    for r in range(2, count + 4):
        raw.append(row(r))
        scaled.append(raw[r] * c_ref[r])
        v = add_stencil(scaled[r - 2], scaled[r - 1], scaled[r], raw[r - 1], one_ref, lanes)
        v = v.astype(jnp.bfloat16).astype(jnp.float32)
        after.append(v)
        after_scaled.append(v * c_ref[r - 1])
        if r >= 4:
            store(
                r - 4,
                add_stencil(
                    after_scaled[r - 3],
                    after_scaled[r - 2],
                    after_scaled[r - 1],
                    after[r - 2],
                    two_ref,
                    lanes,
                ),
            )


def inner_kernel(c_ref, flag_ref, u_ref, a_ref, b_ref, one_ref, two_ref, mixed_ref, side_ref):
    rows, cols, channels = u_ref.shape
    west = flag_ref[0] == 1
    north, south = flag_ref[1], flag_ref[2]

    def chunk(n, _):
        lanes = pl.ds(pl.multiple_of(n * LANES, LANES), LANES)

        def row(r):
            if 2 <= r < rows + 2:
                main = u_ref[r - 2, :, lanes]
            elif r < 2:
                i = jnp.where(north == 1, 1 - r, r)
                main = jnp.where(
                    west,
                    b_ref[i, :, lanes].astype(jnp.float32),
                    a_ref[i, :, lanes].astype(jnp.float32),
                )
            else:
                i = jnp.where(south == 1, rows + 3 - r, r - rows - 2)
                main = jnp.where(
                    west,
                    a_ref[i, :, lanes].astype(jnp.float32),
                    b_ref[i, :, lanes].astype(jnp.float32),
                )
            side_ref[r, :, lanes] = main[cols - 8 :].astype(jnp.bfloat16)
            return main

        def store(r, v):
            mixed_ref[r, :, lanes] = v.astype(jnp.bfloat16)

        two_stencils(row, rows, c_ref, one_ref, two_ref, lanes, store)
        return 0

    lax.fori_loop(0, channels // LANES, chunk, 0)


def inner(c, flags, u, a, b, one, two):
    rows, cols, channels = u.shape
    vmem, smem = pl.BlockSpec(memory_space=pltpu.VMEM), pl.BlockSpec(memory_space=pltpu.SMEM)
    return pl.pallas_call(
        inner_kernel,
        out_shape=(
            jax.ShapeDtypeStruct((rows, cols, channels), jnp.bfloat16),
            jax.ShapeDtypeStruct((rows + 4, 8, channels), jnp.bfloat16),
        ),
        in_specs=[smem, smem] + [vmem] * 5,
        out_specs=(vmem, vmem),
        compiler_params=pltpu.CompilerParams(vmem_limit_bytes=VMEM_LIMIT),
        cost_estimate=pl.CostEstimate(
            flops=40 * rows * cols * channels, bytes_accessed=8 * 1024 * 1024, transcendentals=0
        ),
        name="inner",
    )(c, flags, u, a, b, one, two)


def project_kernel(
    c_ref,
    side_ref,
    edge_ref,
    inner_ref,
    one_ref,
    two_ref,
    gain_ref,
    wkv,
    wq0,
    wq1,
    wq2,
    wq3,
    mixed_hbm,
    slots_hbm,
    head_ref,
    mixed_ref,
    slots_ref,
    strip,
    normed,
    sems,
    slot_sems,
):
    rows, cols, channels = inner_ref.shape
    margin = edge_ref.shape[1]
    pad = jnp.zeros((8 - margin, STRIP_LANES), jnp.float32)

    def chunk(n, _):
        lanes = pl.ds(pl.multiple_of(n * STRIP_LANES, STRIP_LANES), STRIP_LANES)

        def row(r):
            return jnp.concatenate(
                [
                    side_ref[r, :, lanes].astype(jnp.float32),
                    edge_ref[r, :, lanes].astype(jnp.float32),
                    pad,
                ],
                axis=0,
            )

        def store(r, v):
            strip[r, :, lanes] = v

        two_stencils(row, rows, c_ref, one_ref, two_ref, lanes, store)
        return 0

    lax.fori_loop(0, channels // STRIP_LANES, chunk, 0, unroll=UNROLL)
    place = lax.broadcasted_iota(jnp.int32, (8, channels), 0)
    copies = []
    kw = KV_HEADS * HEAD_DIM
    half = rows // 2
    for start in range(0, rows, half):
        for r in range(start, start + half):
            m = inner_ref[r].astype(jnp.float32)
            m = jnp.concatenate(
                [
                    jnp.where(place < MARGIN, strip[r, 8:], m[:8]),
                    m[8 : cols - 8],
                    jnp.where(place >= 8 - MARGIN, strip[r, :8], m[cols - 8 :]),
                ],
                axis=0,
            ).astype(jnp.bfloat16)
            mixed_ref[r] = m
            head_ref[r] = m[: 2 * 8]
            copies.append(pltpu.make_async_copy(mixed_ref.at[r], mixed_hbm.at[r], sems.at[r]))
            copies[-1].start()
            m = m.astype(jnp.float32)
            mean_square = jnp.sum(m * m, axis=1, keepdims=True) * (1.0 / channels)
            normed[r * cols : (r + 1) * cols, :] = (
                m * lax.rsqrt(mean_square + 1e-06) * gain_ref[...]
            ).astype(jnp.bfloat16)
        x = normed[start * cols : (start + half) * cols, :]
        kv = jnp.dot(x, wkv[...], preferred_element_type=jnp.float32).astype(jnp.bfloat16)
        for g, wq in enumerate((wq0, wq1, wq2, wq3)):
            q = jnp.dot(x, wq[...], preferred_element_type=jnp.float32)
            q = (q * (math.log2(math.e) / math.sqrt(HEAD_DIM))).astype(jnp.bfloat16)
            at = g * HEAD_DIM
            pair = jnp.concatenate(
                [kv[:, at : at + HEAD_DIM], kv[:, kw + at : kw + at + HEAD_DIM]], axis=1
            )
            for r in range(half):
                here = slice(r * cols, (r + 1) * cols)
                slots_ref[start + r, g, :, :QW] = q[here]
                slots_ref[start + r, g, :, QW:] = pair[here]
            part = pl.ds(start, half)
            copies.append(
                pltpu.make_async_copy(
                    slots_ref.at[part, g],
                    slots_hbm.at[part, g],
                    slot_sems.at[start // half * KV_HEADS + g],
                )
            )
            copies[-1].start()
    for copy in copies:
        copy.wait()


def project(c, side, edge, mixed, one, two, gain, wq, wkv):
    rows, cols, channels = mixed.shape
    vmem, smem = pl.BlockSpec(memory_space=pltpu.VMEM), pl.BlockSpec(memory_space=pltpu.SMEM)
    hbm = pl.BlockSpec(memory_space=pltpu.HBM)
    return pl.pallas_call(
        project_kernel,
        out_shape=(
            jax.ShapeDtypeStruct((rows, cols, channels), jnp.bfloat16),
            jax.ShapeDtypeStruct((rows, KV_HEADS, cols, SLOT), jnp.bfloat16),
            jax.ShapeDtypeStruct((rows, 16, channels), jnp.bfloat16),
        ),
        in_specs=[smem] + [vmem] * (7 + KV_HEADS),
        out_specs=(hbm, hbm, vmem),
        scratch_shapes=[
            pltpu.VMEM((rows, cols, channels), jnp.bfloat16),
            pltpu.VMEM((rows, KV_HEADS, cols, SLOT), jnp.bfloat16),
            pltpu.VMEM((rows, 16, channels), jnp.float32),
            pltpu.VMEM((rows * cols, channels), jnp.bfloat16),
            pltpu.SemaphoreType.DMA((rows,)),
            pltpu.SemaphoreType.DMA((2 * KV_HEADS,)),
        ],
        compiler_params=pltpu.CompilerParams(vmem_limit_bytes=VMEM_LIMIT),
        cost_estimate=pl.CostEstimate(
            flops=3 * rows * cols * channels * channels,
            bytes_accessed=6 * 1024 * 1024,
            transcendentals=0,
        ),
        name="project",
    )(c, side, edge, mixed, one, two, gain, wkv, *wq)


def attention_kernel(x_ref, o_ref):
    blocks, cols, _ = o_ref.shape
    n = blocks * cols
    kt = x_ref[:, QW : QW + HEAD_DIM].T
    ones = jnp.ones((n, HEAD_DIM), jnp.bfloat16)
    v = jnp.concatenate([x_ref[:, QW + HEAD_DIM :], ones], axis=1)
    step = n // 2
    work = [(i, h) for i in range(0, n, step) for h in range(GROUPS)]

    def scores(i, h):
        q = x_ref[i : i + step, h * HEAD_DIM : (h + 1) * HEAD_DIM]
        return jnp.dot(q, kt, preferred_element_type=jnp.float32)

    outs, ready = [], scores(*work[0])
    for w, (i, h) in enumerate(work):
        s, ready = ready, scores(*work[w + 1]) if w + 1 < len(work) else None
        p = jnp.exp2(s - jnp.max(s, axis=1, keepdims=True)).astype(jnp.bfloat16)
        o = jnp.dot(p, v, preferred_element_type=jnp.float32)
        outs.append(o[:, :HEAD_DIM] / o[:, HEAD_DIM:])
        if h == GROUPS - 1:
            o = jnp.concatenate(outs, axis=1).astype(jnp.bfloat16)
            o_ref[i // cols : (i + step) // cols] = o.reshape(step // cols, cols, QW)
            outs = []
    tile = 16
    heads = [o_ref[b, :tile, :] for b in range(blocks)]
    moved = lax.broadcasted_iota(jnp.int32, (tile, QW), 0) < MARGIN
    for b in range(blocks):
        o_ref[b, :tile, :] = jnp.where(moved, heads[b - 1], heads[b])


def attention(x, blocks):
    n = x.shape[0]
    return pl.pallas_call(
        attention_kernel,
        out_shape=jax.ShapeDtypeStruct((blocks, n // blocks, QW), jnp.bfloat16),
        in_specs=[pl.BlockSpec(memory_space=pltpu.VMEM)],
        out_specs=pl.BlockSpec(memory_space=pltpu.VMEM),
        compiler_params=pltpu.CompilerParams(vmem_limit_bytes=VMEM_LIMIT),
        cost_estimate=pl.CostEstimate(
            flops=4 * GROUPS * n * n * HEAD_DIM,
            bytes_accessed=2 * n * (SLOT + QW),
            transcendentals=GROUPS * n * n,
        ),
        name="attention",
    )(x)


def gather_heads_kernel(x_ref, head_ref, displaced_ref, _, o_hbm, mixed_hbm, staged, tile, sems):
    rows, margin, channels = displaced_ref.shape
    copies = []
    moved = lax.broadcasted_iota(jnp.int32, (16, channels), 0) < margin
    pad = jnp.zeros((16 - margin, channels), jnp.float32)
    for r in range(rows):
        new = jnp.concatenate([displaced_ref[r].astype(jnp.float32), pad], axis=0)
        tile[r] = jnp.where(moved, new, head_ref[r].astype(jnp.float32)).astype(jnp.bfloat16)
        copies.append(
            pltpu.make_async_copy(tile.at[r], mixed_hbm.at[r, pl.ds(0, 16)], sems.at[rows + r])
        )
        copies[-1].start()
        for g in range(KV_HEADS):
            staged[r, :, g * QW : (g + 1) * QW] = x_ref[r * KV_HEADS + g]
        copies.append(pltpu.make_async_copy(staged.at[r], o_hbm.at[r], sems.at[r]))
        copies[-1].start()
    for copy in copies:
        copy.wait()


def gather_heads(x, head, displaced, mixed):
    rows, cols, channels = mixed.shape
    vmem, hbm = pl.BlockSpec(memory_space=pltpu.VMEM), pl.BlockSpec(memory_space=pltpu.HBM)
    whole = jax.ShapeDtypeStruct((rows, cols, channels), jnp.bfloat16)
    return pl.pallas_call(
        gather_heads_kernel,
        out_shape=(whole, whole),
        in_specs=[vmem, vmem, vmem, hbm],
        out_specs=(hbm, hbm),
        input_output_aliases={3: 1},
        scratch_shapes=[
            pltpu.VMEM((rows, cols, channels), jnp.bfloat16),
            pltpu.VMEM((rows, 16, channels), jnp.bfloat16),
            pltpu.SemaphoreType.DMA((2 * rows,)),
        ],
        compiler_params=pltpu.CompilerParams(vmem_limit_bytes=VMEM_LIMIT),
        name="gather_heads",
    )(x, head, displaced, mixed)


def local(grid_state, stencil_one, stencil_two, norm_gain, query_weight, key_value_weight):
    u = grid_state[0]
    rows, cols, channels = u.shape
    bands, columns = lax.axis_size("lat"), lax.axis_size("lon")
    lat, lon = lax.axis_index("lat"), lax.axis_index("lon")
    c = row_weights(lat * rows - 2, rows + 4, rows * bands)
    west = lon < columns // 2
    first, last = lat == 0, lat == bands - 1

    rim_a, rim_b = rims(west.astype(jnp.int32)[None], u)
    rim_a, rim_b, u = lax.optimization_barrier((rim_a, rim_b, u))
    a = lax.ppermute(rim_a, ("lat", "lon"), meridian_pairs(bands, columns, True))
    b = lax.ppermute(rim_b, ("lat", "lon"), meridian_pairs(bands, columns, False))

    ea, eb, eu = a[:, : 2 * MARGIN], b[:, : 2 * MARGIN], u[:, : 2 * MARGIN]
    lower, upper = jnp.where(west, ea, eb), jnp.where(west, eb, ea)
    lower = jnp.where(last, lower[::-1], lower)
    upper = jnp.where(first, upper[::-1], upper)
    edge = lax.ppermute(
        jnp.concatenate([upper, eu, lower], axis=0),
        "lon",
        [(j, (j - 1) % columns) for j in range(columns)],
    )
    flags = jnp.stack([west, first, last]).astype(jnp.int32)
    mixed_inner, side = inner(c, flags, u.astype(jnp.float32), a, b, stencil_one, stencil_two)
    mixed_field, slots, head_tile = project(
        c,
        side,
        edge,
        mixed_inner,
        stencil_one,
        stencil_two,
        norm_gain[None],
        [query_weight[:, g * QW : (g + 1) * QW] for g in range(KV_HEADS)],
        key_value_weight,
    )
    circle = lax.all_to_all(slots.reshape(rows * KV_HEADS, cols, SLOT), "lon", 0, 0, tiled=True)
    displaced = lax.ppermute(
        head_tile[:, :MARGIN], "lon", [(j, (j + 1) % columns) for j in range(columns)]
    )
    circle, displaced = lax.optimization_barrier((circle, displaced))
    back = attention(circle.reshape(-1, SLOT), columns)
    back = lax.all_to_all(back, "lon", 0, 0, tiled=True)
    attended, mixed_field = gather_heads(back, head_tile, displaced, mixed_field)
    return mixed_field[None], attended[None]


def solution(mesh):
    spec = P(None, "lat", "lon", None)
    return jax.shard_map(
        local,
        mesh=mesh,
        in_specs=(spec, P(), P(), P(), P(), P()),
        out_specs=(spec, spec),
        check_vma=False,
    )
```

```python
import math

import jax
import jax.numpy as jnp
from jax import lax
from jax.experimental import pallas as pl
from jax.experimental.pallas import tpu as pltpu
from jax.sharding import PartitionSpec as P

HEADS = 16
KV_HEADS = 4
HEAD_DIM = 64
GROUPS = HEADS // KV_HEADS
QW = GROUPS * HEAD_DIM
SLOT = QW + 2 * HEAD_DIM
MARGIN = 2
STRIP_LANES = 512
UNROLL = 1
LANES = 128
VMEM_LIMIT = 24 * 1024 * 1024


def meridian_pairs(bands, columns, west_north):
    half = columns // 2
    pairs = []
    for i in range(bands):
        for j in range(columns):
            if (j < half) == west_north:
                to = (i - 1, j) if i > 0 else (0, (j + half) % columns)
            else:
                to = (i + 1, j) if i < bands - 1 else (bands - 1, (j + half) % columns)
            pairs.append((i * columns + j, to[0] * columns + to[1]))
    return pairs


def row_weights(first_row, row_count, nlat):
    positions = (jnp.arange(row_count, dtype=jnp.int32) + first_row).astype(jnp.float32)
    return jnp.abs(jnp.sin(jnp.pi * (positions + 0.5) / nlat))


def rims_kernel(west_ref, u_hbm, a_ref, b_ref, sems):
    count = a_ref.shape[0]
    last = u_hbm.shape[0] - count
    west = west_ref[0]
    copies = [
        pltpu.make_async_copy(u_hbm.at[pl.ds(last * (1 - west), count)], a_ref, sems.at[0]),
        pltpu.make_async_copy(u_hbm.at[pl.ds(last * west, count)], b_ref, sems.at[1]),
    ]
    for copy in copies:
        copy.start()
    for copy in copies:
        copy.wait()


def rims(west, u):
    rows, cols, channels = u.shape
    rim = jax.ShapeDtypeStruct((2, cols, channels), jnp.bfloat16)
    vmem = pl.BlockSpec(memory_space=pltpu.VMEM)
    return pl.pallas_call(
        rims_kernel,
        out_shape=(rim, rim),
        in_specs=[pl.BlockSpec(memory_space=pltpu.SMEM), pl.BlockSpec(memory_space=pltpu.HBM)],
        out_specs=(vmem, vmem),
        scratch_shapes=[pltpu.SemaphoreType.DMA((2,))],
        compiler_params=pltpu.CompilerParams(vmem_limit_bytes=VMEM_LIMIT),
        name="rims",
    )(west, u)


def add_stencil(before, here, after, raw, w_ref, lanes):
    beside = before + after
    t = [
        w_ref[0, b : b + 1, lanes] * here + w_ref[1, b : b + 1, lanes] * beside for b in range(3)
    ]
    return raw + t[1] + pltpu.roll(t[0], 1, 0) + pltpu.roll(t[2], raw.shape[0] - 1, 0)


def two_stencils(row, count, c_ref, one_ref, two_ref, lanes, store, known=None):
    raw = [row(0), row(1)]
    scaled = [raw[0] * c_ref[0], raw[1] * c_ref[1]]
    after, after_scaled = [None], [None]
    for r in range(2, count + 4):
        raw.append(row(r))
        scaled.append(raw[r] * c_ref[r])
        if known is not None and 4 <= r < count + 2:
            v = known(r - 4)
        else:
            v = add_stencil(scaled[r - 2], scaled[r - 1], scaled[r], raw[r - 1], one_ref, lanes)
            v = v.astype(jnp.bfloat16).astype(jnp.float32)
        after.append(v)
        after_scaled.append(v * c_ref[r - 1])
        if r >= 4:
            store(
                r - 4,
                add_stencil(
                    after_scaled[r - 3],
                    after_scaled[r - 2],
                    after_scaled[r - 1],
                    after[r - 2],
                    two_ref,
                    lanes,
                ),
            )


def own_rows_kernel(c_ref, u_ref, one_ref, known_ref):
    rows, _, channels = u_ref.shape

    def chunk(n, _):
        lanes = pl.ds(pl.multiple_of(n * LANES, LANES), LANES)
        raw = [u_ref[r, :, lanes] for r in range(rows)]
        scaled = [raw[r] * c_ref[r + 2] for r in range(rows)]
        for r in range(1, rows - 1):
            v = add_stencil(scaled[r - 1], scaled[r], scaled[r + 1], raw[r], one_ref, lanes)
            known_ref[r - 1, :, lanes] = v.astype(jnp.bfloat16)
        return 0

    lax.fori_loop(0, channels // LANES, chunk, 0)


def own_rows(c, u, one):
    rows, cols, channels = u.shape
    vmem, smem = pl.BlockSpec(memory_space=pltpu.VMEM), pl.BlockSpec(memory_space=pltpu.SMEM)
    return pl.pallas_call(
        own_rows_kernel,
        out_shape=jax.ShapeDtypeStruct((rows - 2, cols, channels), jnp.bfloat16),
        in_specs=[smem, vmem, vmem],
        out_specs=vmem,
        compiler_params=pltpu.CompilerParams(vmem_limit_bytes=VMEM_LIMIT),
        cost_estimate=pl.CostEstimate(
            flops=8 * rows * cols * channels, bytes_accessed=1024 * 1024, transcendentals=0
        ),
        name="own_rows",
    )(c, u, one)


def inner_kernel(
    c_ref, flag_ref, u_ref, known_ref, a_ref, b_ref, one_ref, two_ref, mixed_ref, side_ref
):
    rows, cols, channels = u_ref.shape
    west = flag_ref[0] == 1
    north, south = flag_ref[1], flag_ref[2]

    def chunk(n, _):
        lanes = pl.ds(pl.multiple_of(n * LANES, LANES), LANES)

        def row(r):
            if 2 <= r < rows + 2:
                main = u_ref[r - 2, :, lanes]
            elif r < 2:
                i = jnp.where(north == 1, 1 - r, r)
                main = jnp.where(
                    west,
                    b_ref[i, :, lanes].astype(jnp.float32),
                    a_ref[i, :, lanes].astype(jnp.float32),
                )
            else:
                i = jnp.where(south == 1, rows + 3 - r, r - rows - 2)
                main = jnp.where(
                    west,
                    a_ref[i, :, lanes].astype(jnp.float32),
                    b_ref[i, :, lanes].astype(jnp.float32),
                )
            side_ref[r, :, lanes] = main[cols - 8 :].astype(jnp.bfloat16)
            return main

        def store(r, v):
            mixed_ref[r, :, lanes] = v.astype(jnp.bfloat16)

        def known(r):
            return known_ref[r, :, lanes].astype(jnp.float32)

        two_stencils(row, rows, c_ref, one_ref, two_ref, lanes, store, known)
        return 0

    lax.fori_loop(0, channels // LANES, chunk, 0)


def inner(c, flags, u, known, a, b, one, two):
    rows, cols, channels = u.shape
    vmem, smem = pl.BlockSpec(memory_space=pltpu.VMEM), pl.BlockSpec(memory_space=pltpu.SMEM)
    return pl.pallas_call(
        inner_kernel,
        out_shape=(
            jax.ShapeDtypeStruct((rows, cols, channels), jnp.bfloat16),
            jax.ShapeDtypeStruct((rows + 4, 8, channels), jnp.bfloat16),
        ),
        in_specs=[smem, smem] + [vmem] * 6,
        out_specs=(vmem, vmem),
        compiler_params=pltpu.CompilerParams(vmem_limit_bytes=VMEM_LIMIT),
        cost_estimate=pl.CostEstimate(
            flops=40 * rows * cols * channels, bytes_accessed=8 * 1024 * 1024, transcendentals=0
        ),
        name="inner",
    )(c, flags, u, known, a, b, one, two)


def project_kernel(
    c_ref,
    side_ref,
    edge_ref,
    inner_ref,
    one_ref,
    two_ref,
    gain_ref,
    wkv,
    wq0,
    wq1,
    wq2,
    wq3,
    mixed_hbm,
    slots_hbm,
    head_ref,
    mixed_ref,
    slots_ref,
    strip,
    normed,
    sems,
    slot_sems,
):
    rows, cols, channels = inner_ref.shape
    margin = edge_ref.shape[1]
    pad = jnp.zeros((8 - margin, STRIP_LANES), jnp.float32)

    def chunk(n, _):
        lanes = pl.ds(pl.multiple_of(n * STRIP_LANES, STRIP_LANES), STRIP_LANES)

        def row(r):
            return jnp.concatenate(
                [
                    side_ref[r, :, lanes].astype(jnp.float32),
                    edge_ref[r, :, lanes].astype(jnp.float32),
                    pad,
                ],
                axis=0,
            )

        def store(r, v):
            strip[r, :, lanes] = v

        two_stencils(row, rows, c_ref, one_ref, two_ref, lanes, store)
        return 0

    lax.fori_loop(0, channels // STRIP_LANES, chunk, 0, unroll=UNROLL)
    place = lax.broadcasted_iota(jnp.int32, (8, channels), 0)
    copies = []
    kw = KV_HEADS * HEAD_DIM
    half = rows // 2
    for start in range(0, rows, half):
        for r in range(start, start + half):
            m = inner_ref[r].astype(jnp.float32)
            m = jnp.concatenate(
                [
                    jnp.where(place < MARGIN, strip[r, 8:], m[:8]),
                    m[8 : cols - 8],
                    jnp.where(place >= 8 - MARGIN, strip[r, :8], m[cols - 8 :]),
                ],
                axis=0,
            ).astype(jnp.bfloat16)
            mixed_ref[r] = m
            head_ref[r] = m[: 2 * 8]
            copies.append(pltpu.make_async_copy(mixed_ref.at[r], mixed_hbm.at[r], sems.at[r]))
            copies[-1].start()
            m = m.astype(jnp.float32)
            mean_square = jnp.sum(m * m, axis=1, keepdims=True) * (1.0 / channels)
            normed[r * cols : (r + 1) * cols, :] = (
                m * lax.rsqrt(mean_square + 1e-06) * gain_ref[...]
            ).astype(jnp.bfloat16)
        x = normed[start * cols : (start + half) * cols, :]
        kv = jnp.dot(x, wkv[...], preferred_element_type=jnp.float32).astype(jnp.bfloat16)
        for g, wq in enumerate((wq0, wq1, wq2, wq3)):
            q = jnp.dot(x, wq[...], preferred_element_type=jnp.float32)
            q = (q * (math.log2(math.e) / math.sqrt(HEAD_DIM))).astype(jnp.bfloat16)
            at = g * HEAD_DIM
            pair = jnp.concatenate(
                [kv[:, at : at + HEAD_DIM], kv[:, kw + at : kw + at + HEAD_DIM]], axis=1
            )
            for r in range(half):
                here = slice(r * cols, (r + 1) * cols)
                slots_ref[start + r, g, :, :QW] = q[here]
                slots_ref[start + r, g, :, QW:] = pair[here]
            part = pl.ds(start, half)
            copies.append(
                pltpu.make_async_copy(
                    slots_ref.at[part, g],
                    slots_hbm.at[part, g],
                    slot_sems.at[start // half * KV_HEADS + g],
                )
            )
            copies[-1].start()
    for copy in copies:
        copy.wait()


def project(c, side, edge, mixed, one, two, gain, wq, wkv):
    rows, cols, channels = mixed.shape
    vmem, smem = pl.BlockSpec(memory_space=pltpu.VMEM), pl.BlockSpec(memory_space=pltpu.SMEM)
    hbm = pl.BlockSpec(memory_space=pltpu.HBM)
    return pl.pallas_call(
        project_kernel,
        out_shape=(
            jax.ShapeDtypeStruct((rows, cols, channels), jnp.bfloat16),
            jax.ShapeDtypeStruct((rows, KV_HEADS, cols, SLOT), jnp.bfloat16),
            jax.ShapeDtypeStruct((rows, 16, channels), jnp.bfloat16),
        ),
        in_specs=[smem] + [vmem] * (7 + KV_HEADS),
        out_specs=(hbm, hbm, vmem),
        scratch_shapes=[
            pltpu.VMEM((rows, cols, channels), jnp.bfloat16),
            pltpu.VMEM((rows, KV_HEADS, cols, SLOT), jnp.bfloat16),
            pltpu.VMEM((rows, 16, channels), jnp.float32),
            pltpu.VMEM((rows * cols, channels), jnp.bfloat16),
            pltpu.SemaphoreType.DMA((rows,)),
            pltpu.SemaphoreType.DMA((2 * KV_HEADS,)),
        ],
        compiler_params=pltpu.CompilerParams(vmem_limit_bytes=VMEM_LIMIT),
        cost_estimate=pl.CostEstimate(
            flops=3 * rows * cols * channels * channels,
            bytes_accessed=6 * 1024 * 1024,
            transcendentals=0,
        ),
        name="project",
    )(c, side, edge, mixed, one, two, gain, wkv, *wq)


def attention_kernel(x_ref, o_ref):
    blocks, cols, _ = o_ref.shape
    n = blocks * cols
    kt = x_ref[:, QW : QW + HEAD_DIM].T
    ones = jnp.ones((n, HEAD_DIM), jnp.bfloat16)
    v = jnp.concatenate([x_ref[:, QW + HEAD_DIM :], ones], axis=1)
    step = n // 2
    work = [(i, h) for i in range(0, n, step) for h in range(GROUPS)]

    def scores(i, h):
        q = x_ref[i : i + step, h * HEAD_DIM : (h + 1) * HEAD_DIM]
        return jnp.dot(q, kt, preferred_element_type=jnp.float32)

    outs, ready = [], scores(*work[0])
    for w, (i, h) in enumerate(work):
        s, ready = ready, scores(*work[w + 1]) if w + 1 < len(work) else None
        p = jnp.exp2(s - jnp.max(s, axis=1, keepdims=True)).astype(jnp.bfloat16)
        o = jnp.dot(p, v, preferred_element_type=jnp.float32)
        outs.append(o[:, :HEAD_DIM] / o[:, HEAD_DIM:])
        if h == GROUPS - 1:
            o = jnp.concatenate(outs, axis=1).astype(jnp.bfloat16)
            o_ref[i // cols : (i + step) // cols] = o.reshape(step // cols, cols, QW)
            outs = []
    tile = 16
    heads = [o_ref[b, :tile, :] for b in range(blocks)]
    moved = lax.broadcasted_iota(jnp.int32, (tile, QW), 0) < MARGIN
    for b in range(blocks):
        o_ref[b, :tile, :] = jnp.where(moved, heads[b - 1], heads[b])


def attention(x, blocks):
    n = x.shape[0]
    return pl.pallas_call(
        attention_kernel,
        out_shape=jax.ShapeDtypeStruct((blocks, n // blocks, QW), jnp.bfloat16),
        in_specs=[pl.BlockSpec(memory_space=pltpu.VMEM)],
        out_specs=pl.BlockSpec(memory_space=pltpu.VMEM),
        compiler_params=pltpu.CompilerParams(vmem_limit_bytes=VMEM_LIMIT),
        cost_estimate=pl.CostEstimate(
            flops=4 * GROUPS * n * n * HEAD_DIM,
            bytes_accessed=2 * n * (SLOT + QW),
            transcendentals=GROUPS * n * n,
        ),
        name="attention",
    )(x)


def gather_heads_kernel(x_ref, head_ref, displaced_ref, _, o_hbm, mixed_hbm, staged, tile, sems):
    rows, margin, channels = displaced_ref.shape
    copies = []
    moved = lax.broadcasted_iota(jnp.int32, (16, channels), 0) < margin
    pad = jnp.zeros((16 - margin, channels), jnp.float32)
    for r in range(rows):
        new = jnp.concatenate([displaced_ref[r].astype(jnp.float32), pad], axis=0)
        tile[r] = jnp.where(moved, new, head_ref[r].astype(jnp.float32)).astype(jnp.bfloat16)
        copies.append(
            pltpu.make_async_copy(tile.at[r], mixed_hbm.at[r, pl.ds(0, 16)], sems.at[rows + r])
        )
        copies[-1].start()
        for g in range(KV_HEADS):
            staged[r, :, g * QW : (g + 1) * QW] = x_ref[r * KV_HEADS + g]
        copies.append(pltpu.make_async_copy(staged.at[r], o_hbm.at[r], sems.at[r]))
        copies[-1].start()
    for copy in copies:
        copy.wait()


def gather_heads(x, head, displaced, mixed):
    rows, cols, channels = mixed.shape
    vmem, hbm = pl.BlockSpec(memory_space=pltpu.VMEM), pl.BlockSpec(memory_space=pltpu.HBM)
    whole = jax.ShapeDtypeStruct((rows, cols, channels), jnp.bfloat16)
    return pl.pallas_call(
        gather_heads_kernel,
        out_shape=(whole, whole),
        in_specs=[vmem, vmem, vmem, hbm],
        out_specs=(hbm, hbm),
        input_output_aliases={3: 1},
        scratch_shapes=[
            pltpu.VMEM((rows, cols, channels), jnp.bfloat16),
            pltpu.VMEM((rows, 16, channels), jnp.bfloat16),
            pltpu.SemaphoreType.DMA((2 * rows,)),
        ],
        compiler_params=pltpu.CompilerParams(vmem_limit_bytes=VMEM_LIMIT),
        name="gather_heads",
    )(x, head, displaced, mixed)


def local(grid_state, stencil_one, stencil_two, norm_gain, query_weight, key_value_weight):
    u = grid_state[0]
    rows, cols, channels = u.shape
    bands, columns = lax.axis_size("lat"), lax.axis_size("lon")
    lat, lon = lax.axis_index("lat"), lax.axis_index("lon")
    c = row_weights(lat * rows - 2, rows + 4, rows * bands)
    west = lon < columns // 2
    first, last = lat == 0, lat == bands - 1

    rim_a, rim_b = rims(west.astype(jnp.int32)[None], u)
    rim_a, rim_b, u = lax.optimization_barrier((rim_a, rim_b, u))
    a = lax.ppermute(rim_a, ("lat", "lon"), meridian_pairs(bands, columns, True))
    b = lax.ppermute(rim_b, ("lat", "lon"), meridian_pairs(bands, columns, False))

    ea, eb, eu = a[:, : 2 * MARGIN], b[:, : 2 * MARGIN], u[:, : 2 * MARGIN]
    lower, upper = jnp.where(west, ea, eb), jnp.where(west, eb, ea)
    lower = jnp.where(last, lower[::-1], lower)
    upper = jnp.where(first, upper[::-1], upper)
    edge = lax.ppermute(
        jnp.concatenate([upper, eu, lower], axis=0),
        "lon",
        [(j, (j - 1) % columns) for j in range(columns)],
    )
    wide = u.astype(jnp.float32)
    flags = jnp.stack([west, first, last]).astype(jnp.int32)
    mixed_inner, side = inner(
        c, flags, wide, own_rows(c, wide, stencil_one), a, b, stencil_one, stencil_two
    )
    mixed_field, slots, head_tile = project(
        c,
        side,
        edge,
        mixed_inner,
        stencil_one,
        stencil_two,
        norm_gain[None],
        [query_weight[:, g * QW : (g + 1) * QW] for g in range(KV_HEADS)],
        key_value_weight,
    )
    circle = lax.all_to_all(slots.reshape(rows * KV_HEADS, cols, SLOT), "lon", 0, 0, tiled=True)
    displaced = lax.ppermute(
        head_tile[:, :MARGIN], "lon", [(j, (j + 1) % columns) for j in range(columns)]
    )
    circle, displaced = lax.optimization_barrier((circle, displaced))
    back = attention(circle.reshape(-1, SLOT), columns)
    back = lax.all_to_all(back, "lon", 0, 0, tiled=True)
    attended, mixed_field = gather_heads(back, head_tile, displaced, mixed_field)
    return mixed_field[None], attended[None]


def solution(mesh):
    spec = P(None, "lat", "lon", None)
    return jax.shard_map(
        local,
        mesh=mesh,
        in_specs=(spec, P(), P(), P(), P(), P()),
        out_specs=(spec, spec),
        check_vma=False,
    )
```

```python
import math

import jax
import jax.numpy as jnp
from jax import lax
from jax.experimental import pallas as pl
from jax.experimental.pallas import tpu as pltpu
from jax.sharding import PartitionSpec as P

HEADS = 16
KV_HEADS = 4
HEAD_DIM = 64
GROUPS = HEADS // KV_HEADS
QW = GROUPS * HEAD_DIM
SLOT = QW + 2 * HEAD_DIM
MARGIN = 2
STRIP_LANES = 512
UNROLL = 1
LANES = 128
VMEM_LIMIT = 24 * 1024 * 1024


def meridian_pairs(bands, columns, west_north):
    half = columns // 2
    pairs = []
    for i in range(bands):
        for j in range(columns):
            if (j < half) == west_north:
                to = (i - 1, j) if i > 0 else (0, (j + half) % columns)
            else:
                to = (i + 1, j) if i < bands - 1 else (bands - 1, (j + half) % columns)
            pairs.append((i * columns + j, to[0] * columns + to[1]))
    return pairs


def row_weights(first_row, row_count, nlat):
    positions = (jnp.arange(row_count, dtype=jnp.int32) + first_row).astype(jnp.float32)
    return jnp.abs(jnp.sin(jnp.pi * (positions + 0.5) / nlat))


def rims_kernel(west_ref, u_hbm, a_ref, b_ref, sems):
    count = a_ref.shape[0]
    last = u_hbm.shape[0] - count
    west = west_ref[0]
    copies = [
        pltpu.make_async_copy(u_hbm.at[pl.ds(last * (1 - west), count)], a_ref, sems.at[0]),
        pltpu.make_async_copy(u_hbm.at[pl.ds(last * west, count)], b_ref, sems.at[1]),
    ]
    for copy in copies:
        copy.start()
    for copy in copies:
        copy.wait()


def rims(west, u):
    rows, cols, channels = u.shape
    rim = jax.ShapeDtypeStruct((2, cols, channels), jnp.bfloat16)
    vmem = pl.BlockSpec(memory_space=pltpu.VMEM)
    return pl.pallas_call(
        rims_kernel,
        out_shape=(rim, rim),
        in_specs=[pl.BlockSpec(memory_space=pltpu.SMEM), pl.BlockSpec(memory_space=pltpu.HBM)],
        out_specs=(vmem, vmem),
        scratch_shapes=[pltpu.SemaphoreType.DMA((2,))],
        compiler_params=pltpu.CompilerParams(vmem_limit_bytes=VMEM_LIMIT),
        name="rims",
    )(west, u)


def add_stencil(before, here, after, raw, w_ref, lanes):
    beside = before + after
    t = [
        w_ref[0, b : b + 1, lanes] * here + w_ref[1, b : b + 1, lanes] * beside for b in range(3)
    ]
    return raw + t[1] + pltpu.roll(t[0], 1, 0) + pltpu.roll(t[2], raw.shape[0] - 1, 0)


def two_stencils(row, count, c_ref, one_ref, two_ref, lanes, store, known=None):
    raw = [row(0), row(1)]
    scaled = [raw[0] * c_ref[0], raw[1] * c_ref[1]]
    after, after_scaled = [None], [None]
    for r in range(2, count + 4):
        raw.append(row(r))
        scaled.append(raw[r] * c_ref[r])
        if known is not None and 4 <= r < count + 2:
            v = known(r - 4)
        else:
            v = add_stencil(scaled[r - 2], scaled[r - 1], scaled[r], raw[r - 1], one_ref, lanes)
            v = v.astype(jnp.bfloat16).astype(jnp.float32)
        after.append(v)
        after_scaled.append(v * c_ref[r - 1])
        if r >= 4:
            store(
                r - 4,
                add_stencil(
                    after_scaled[r - 3],
                    after_scaled[r - 2],
                    after_scaled[r - 1],
                    after[r - 2],
                    two_ref,
                    lanes,
                ),
            )


def own_rows_kernel(c_ref, u_ref, one_ref, known_ref):
    rows, _, channels = u_ref.shape

    def chunk(n, _):
        lanes = pl.ds(pl.multiple_of(n * LANES, LANES), LANES)
        raw = [u_ref[r, :, lanes] for r in range(rows)]
        scaled = [raw[r] * c_ref[r + 2] for r in range(rows)]
        for r in range(1, rows - 1):
            v = add_stencil(scaled[r - 1], scaled[r], scaled[r + 1], raw[r], one_ref, lanes)
            known_ref[r - 1, :, lanes] = v.astype(jnp.bfloat16)
        return 0

    lax.fori_loop(0, channels // LANES, chunk, 0)


def own_rows(c, u, one):
    rows, cols, channels = u.shape
    vmem, smem = pl.BlockSpec(memory_space=pltpu.VMEM), pl.BlockSpec(memory_space=pltpu.SMEM)
    return pl.pallas_call(
        own_rows_kernel,
        out_shape=jax.ShapeDtypeStruct((rows - 2, cols, channels), jnp.bfloat16),
        in_specs=[smem, vmem, vmem],
        out_specs=vmem,
        compiler_params=pltpu.CompilerParams(vmem_limit_bytes=VMEM_LIMIT),
        cost_estimate=pl.CostEstimate(
            flops=8 * rows * cols * channels, bytes_accessed=1024 * 1024, transcendentals=0
        ),
        name="own_rows",
    )(c, u, one)


def inner_kernel(
    c_ref, flag_ref, u_ref, known_ref, a_ref, b_ref, one_ref, two_ref, mixed_ref, side_ref
):
    rows, cols, channels = u_ref.shape
    west = flag_ref[0] == 1
    north, south = flag_ref[1], flag_ref[2]

    def chunk(n, _):
        lanes = pl.ds(pl.multiple_of(n * LANES, LANES), LANES)

        def row(r):
            if 2 <= r < rows + 2:
                main = u_ref[r - 2, :, lanes]
            elif r < 2:
                i = jnp.where(north == 1, 1 - r, r)
                main = jnp.where(
                    west,
                    b_ref[i, :, lanes].astype(jnp.float32),
                    a_ref[i, :, lanes].astype(jnp.float32),
                )
            else:
                i = jnp.where(south == 1, rows + 3 - r, r - rows - 2)
                main = jnp.where(
                    west,
                    a_ref[i, :, lanes].astype(jnp.float32),
                    b_ref[i, :, lanes].astype(jnp.float32),
                )
            side_ref[r, :, lanes] = main[cols - 8 :].astype(jnp.bfloat16)
            return main

        def store(r, v):
            mixed_ref[r, :, lanes] = v.astype(jnp.bfloat16)

        def known(r):
            return known_ref[r, :, lanes].astype(jnp.float32)

        two_stencils(row, rows, c_ref, one_ref, two_ref, lanes, store, known)
        return 0

    lax.fori_loop(0, channels // LANES, chunk, 0)


def inner(c, flags, u, known, a, b, one, two):
    rows, cols, channels = u.shape
    vmem, smem = pl.BlockSpec(memory_space=pltpu.VMEM), pl.BlockSpec(memory_space=pltpu.SMEM)
    return pl.pallas_call(
        inner_kernel,
        out_shape=(
            jax.ShapeDtypeStruct((rows, cols, channels), jnp.bfloat16),
            jax.ShapeDtypeStruct((rows + 4, 8, channels), jnp.bfloat16),
        ),
        in_specs=[smem, smem] + [vmem] * 6,
        out_specs=(vmem, vmem),
        compiler_params=pltpu.CompilerParams(vmem_limit_bytes=VMEM_LIMIT),
        cost_estimate=pl.CostEstimate(
            flops=40 * rows * cols * channels, bytes_accessed=8 * 1024 * 1024, transcendentals=0
        ),
        name="inner",
    )(c, flags, u, known, a, b, one, two)


def project_kernel(
    c_ref,
    side_ref,
    edge_ref,
    inner_ref,
    one_ref,
    two_ref,
    gain_ref,
    wkv,
    wq0,
    wq1,
    wq2,
    wq3,
    mixed_ref,
    slots_hbm,
    head_ref,
    slots_ref,
    strip,
    normed,
    slot_sems,
):
    rows, cols, channels = inner_ref.shape
    margin = edge_ref.shape[1]
    pad = jnp.zeros((8 - margin, STRIP_LANES), jnp.float32)

    def chunk(n, _):
        lanes = pl.ds(pl.multiple_of(n * STRIP_LANES, STRIP_LANES), STRIP_LANES)

        def row(r):
            return jnp.concatenate(
                [
                    side_ref[r, :, lanes].astype(jnp.float32),
                    edge_ref[r, :, lanes].astype(jnp.float32),
                    pad,
                ],
                axis=0,
            )

        def store(r, v):
            strip[r, :, lanes] = v

        two_stencils(row, rows, c_ref, one_ref, two_ref, lanes, store)
        return 0

    lax.fori_loop(0, channels // STRIP_LANES, chunk, 0, unroll=UNROLL)
    place = lax.broadcasted_iota(jnp.int32, (8, channels), 0)
    copies = []
    kw = KV_HEADS * HEAD_DIM
    half = rows // 2
    for start in range(0, rows, half):
        for r in range(start, start + half):
            m = inner_ref[r].astype(jnp.float32)
            m = jnp.concatenate(
                [
                    jnp.where(place < MARGIN, strip[r, 8:], m[:8]),
                    m[8 : cols - 8],
                    jnp.where(place >= 8 - MARGIN, strip[r, :8], m[cols - 8 :]),
                ],
                axis=0,
            ).astype(jnp.bfloat16)
            mixed_ref[r] = m
            head_ref[r] = m[: 2 * 8]
            m = m.astype(jnp.float32)
            mean_square = jnp.sum(m * m, axis=1, keepdims=True) * (1.0 / channels)
            normed[r * cols : (r + 1) * cols, :] = (
                m * lax.rsqrt(mean_square + 1e-06) * gain_ref[...]
            ).astype(jnp.bfloat16)
        x = normed[start * cols : (start + half) * cols, :]
        kv = jnp.dot(x, wkv[...], preferred_element_type=jnp.float32).astype(jnp.bfloat16)
        for g, wq in enumerate((wq0, wq1, wq2, wq3)):
            q = jnp.dot(x, wq[...], preferred_element_type=jnp.float32)
            q = (q * (math.log2(math.e) / math.sqrt(HEAD_DIM))).astype(jnp.bfloat16)
            at = g * HEAD_DIM
            pair = jnp.concatenate(
                [kv[:, at : at + HEAD_DIM], kv[:, kw + at : kw + at + HEAD_DIM]], axis=1
            )
            for r in range(half):
                here = slice(r * cols, (r + 1) * cols)
                slots_ref[start + r, g, :, :QW] = q[here]
                slots_ref[start + r, g, :, QW:] = pair[here]
            part = pl.ds(start, half)
            copies.append(
                pltpu.make_async_copy(
                    slots_ref.at[part, g],
                    slots_hbm.at[part, g],
                    slot_sems.at[start // half * KV_HEADS + g],
                )
            )
            copies[-1].start()
    for copy in copies:
        copy.wait()


def project(c, side, edge, mixed, one, two, gain, wq, wkv):
    rows, cols, channels = mixed.shape
    vmem, smem = pl.BlockSpec(memory_space=pltpu.VMEM), pl.BlockSpec(memory_space=pltpu.SMEM)
    hbm = pl.BlockSpec(memory_space=pltpu.HBM)
    return pl.pallas_call(
        project_kernel,
        out_shape=(
            jax.ShapeDtypeStruct((rows, cols, channels), jnp.bfloat16),
            jax.ShapeDtypeStruct((rows, KV_HEADS, cols, SLOT), jnp.bfloat16),
            jax.ShapeDtypeStruct((rows, 16, channels), jnp.bfloat16),
        ),
        in_specs=[smem] + [vmem] * (7 + KV_HEADS),
        out_specs=(vmem, hbm, vmem),
        scratch_shapes=[
            pltpu.VMEM((rows, KV_HEADS, cols, SLOT), jnp.bfloat16),
            pltpu.VMEM((rows, 16, channels), jnp.float32),
            pltpu.VMEM((rows * cols, channels), jnp.bfloat16),
            pltpu.SemaphoreType.DMA((2 * KV_HEADS,)),
        ],
        compiler_params=pltpu.CompilerParams(vmem_limit_bytes=VMEM_LIMIT),
        cost_estimate=pl.CostEstimate(
            flops=3 * rows * cols * channels * channels,
            bytes_accessed=6 * 1024 * 1024,
            transcendentals=0,
        ),
        name="project",
    )(c, side, edge, mixed, one, two, gain, wkv, *wq)


def attention_kernel(x_ref, mixed_ref, o_ref, mixed_hbm, sem):
    copy = pltpu.make_async_copy(mixed_ref, mixed_hbm, sem)
    copy.start()
    blocks, cols, _ = o_ref.shape
    n = blocks * cols
    kt = x_ref[:, QW : QW + HEAD_DIM].T
    ones = jnp.ones((n, HEAD_DIM), jnp.bfloat16)
    v = jnp.concatenate([x_ref[:, QW + HEAD_DIM :], ones], axis=1)
    step = n // 2
    work = [(i, h) for i in range(0, n, step) for h in range(GROUPS)]

    def scores(i, h):
        q = x_ref[i : i + step, h * HEAD_DIM : (h + 1) * HEAD_DIM]
        return jnp.dot(q, kt, preferred_element_type=jnp.float32)

    outs, ready = [], scores(*work[0])
    for w, (i, h) in enumerate(work):
        s, ready = ready, scores(*work[w + 1]) if w + 1 < len(work) else None
        p = jnp.exp2(s - jnp.max(s, axis=1, keepdims=True)).astype(jnp.bfloat16)
        o = jnp.dot(p, v, preferred_element_type=jnp.float32)
        outs.append(o[:, :HEAD_DIM] / o[:, HEAD_DIM:])
        if h == GROUPS - 1:
            o = jnp.concatenate(outs, axis=1).astype(jnp.bfloat16)
            o_ref[i // cols : (i + step) // cols] = o.reshape(step // cols, cols, QW)
            outs = []
    tile = 16
    heads = [o_ref[b, :tile, :] for b in range(blocks)]
    moved = lax.broadcasted_iota(jnp.int32, (tile, QW), 0) < MARGIN
    for b in range(blocks):
        o_ref[b, :tile, :] = jnp.where(moved, heads[b - 1], heads[b])
    copy.wait()


def attention(x, mixed, blocks):
    n = x.shape[0]
    return pl.pallas_call(
        attention_kernel,
        out_shape=(
            jax.ShapeDtypeStruct((blocks, n // blocks, QW), jnp.bfloat16),
            jax.ShapeDtypeStruct(mixed.shape, mixed.dtype),
        ),
        in_specs=[pl.BlockSpec(memory_space=pltpu.VMEM)] * 2,
        out_specs=(
            pl.BlockSpec(memory_space=pltpu.VMEM),
            pl.BlockSpec(memory_space=pltpu.HBM),
        ),
        scratch_shapes=[pltpu.SemaphoreType.DMA],
        compiler_params=pltpu.CompilerParams(vmem_limit_bytes=VMEM_LIMIT),
        cost_estimate=pl.CostEstimate(
            flops=4 * GROUPS * n * n * HEAD_DIM,
            bytes_accessed=2 * n * (SLOT + QW),
            transcendentals=GROUPS * n * n,
        ),
        name="attention",
    )(x, mixed)


def gather_heads_kernel(x_ref, head_ref, displaced_ref, _, o_hbm, mixed_hbm, staged, tile, sems):
    rows, margin, channels = displaced_ref.shape
    copies = []
    moved = lax.broadcasted_iota(jnp.int32, (16, channels), 0) < margin
    pad = jnp.zeros((16 - margin, channels), jnp.float32)
    for r in range(rows):
        new = jnp.concatenate([displaced_ref[r].astype(jnp.float32), pad], axis=0)
        tile[r] = jnp.where(moved, new, head_ref[r].astype(jnp.float32)).astype(jnp.bfloat16)
        copies.append(
            pltpu.make_async_copy(tile.at[r], mixed_hbm.at[r, pl.ds(0, 16)], sems.at[rows + r])
        )
        copies[-1].start()
        for g in range(KV_HEADS):
            staged[r, :, g * QW : (g + 1) * QW] = x_ref[r * KV_HEADS + g]
        copies.append(pltpu.make_async_copy(staged.at[r], o_hbm.at[r], sems.at[r]))
        copies[-1].start()
    for copy in copies:
        copy.wait()


def gather_heads(x, head, displaced, mixed):
    rows, cols, channels = mixed.shape
    vmem, hbm = pl.BlockSpec(memory_space=pltpu.VMEM), pl.BlockSpec(memory_space=pltpu.HBM)
    whole = jax.ShapeDtypeStruct((rows, cols, channels), jnp.bfloat16)
    return pl.pallas_call(
        gather_heads_kernel,
        out_shape=(whole, whole),
        in_specs=[vmem, vmem, vmem, hbm],
        out_specs=(hbm, hbm),
        input_output_aliases={3: 1},
        scratch_shapes=[
            pltpu.VMEM((rows, cols, channels), jnp.bfloat16),
            pltpu.VMEM((rows, 16, channels), jnp.bfloat16),
            pltpu.SemaphoreType.DMA((2 * rows,)),
        ],
        compiler_params=pltpu.CompilerParams(vmem_limit_bytes=VMEM_LIMIT),
        name="gather_heads",
    )(x, head, displaced, mixed)


def local(grid_state, stencil_one, stencil_two, norm_gain, query_weight, key_value_weight):
    u = grid_state[0]
    rows, cols, channels = u.shape
    bands, columns = lax.axis_size("lat"), lax.axis_size("lon")
    lat, lon = lax.axis_index("lat"), lax.axis_index("lon")
    c = row_weights(lat * rows - 2, rows + 4, rows * bands)
    west = lon < columns // 2
    first, last = lat == 0, lat == bands - 1

    rim_a, rim_b = rims(west.astype(jnp.int32)[None], u)
    rim_a, rim_b, u = lax.optimization_barrier((rim_a, rim_b, u))
    a = lax.ppermute(rim_a, ("lat", "lon"), meridian_pairs(bands, columns, True))
    b = lax.ppermute(rim_b, ("lat", "lon"), meridian_pairs(bands, columns, False))

    ea, eb, eu = a[:, : 2 * MARGIN], b[:, : 2 * MARGIN], u[:, : 2 * MARGIN]
    lower, upper = jnp.where(west, ea, eb), jnp.where(west, eb, ea)
    lower = jnp.where(last, lower[::-1], lower)
    upper = jnp.where(first, upper[::-1], upper)
    edge = lax.ppermute(
        jnp.concatenate([upper, eu, lower], axis=0),
        "lon",
        [(j, (j - 1) % columns) for j in range(columns)],
    )
    wide = u.astype(jnp.float32)
    flags = jnp.stack([west, first, last]).astype(jnp.int32)
    mixed_inner, side = inner(
        c, flags, wide, own_rows(c, wide, stencil_one), a, b, stencil_one, stencil_two
    )
    mixed_field, slots, head_tile = project(
        c,
        side,
        edge,
        mixed_inner,
        stencil_one,
        stencil_two,
        norm_gain[None],
        [query_weight[:, g * QW : (g + 1) * QW] for g in range(KV_HEADS)],
        key_value_weight,
    )
    circle = lax.all_to_all(slots.reshape(rows * KV_HEADS, cols, SLOT), "lon", 0, 0, tiled=True)
    displaced = lax.ppermute(
        head_tile[:, :MARGIN], "lon", [(j, (j + 1) % columns) for j in range(columns)]
    )
    circle, displaced = lax.optimization_barrier((circle, displaced))
    back, mixed_field = attention(circle.reshape(-1, SLOT), mixed_field, columns)
    back = lax.all_to_all(back, "lon", 0, 0, tiled=True)
    attended, mixed_field = gather_heads(back, head_tile, displaced, mixed_field)
    return mixed_field[None], attended[None]


def solution(mesh):
    spec = P(None, "lat", "lon", None)
    return jax.shard_map(
        local,
        mesh=mesh,
        in_specs=(spec, P(), P(), P(), P(), P()),
        out_specs=(spec, spec),
        check_vma=False,
    )
```
